32 devices in a mesh: mol: 2 (over x), tile: 8 (over z, y), rep: 2 (over core).
Axes of the slice: x: 2, y: 2, z: 4, core: 2. Of those that a mesh axis runs over, the one named last changes fastest.
Arguments:
- tasks: int32 [2, 8192], P(None, ('mol', 'tile')), parts along dimension 1, may hold values from 0 to 7, as said below
- task_count: int32 [16], P(('mol', 'tile')), parts along dimension 0, may hold values from 64 to 512, as said below
- integrals: float32 [8192, 4096], P(('mol', 'tile')), parts along dimension 0, may hold values from -0.1875 to 0.1875
- amplitudes: float32 [400, 64, 768], P(('mol', 'tile'), None, 'rep'), parts along dimension 0, may hold values from -6 to 6
- amp_slot: int32 [400], P('mol'), parts along dimension 0, may hold values from 0 to 199, as said below
- need_amp: int32 [128], P(('mol', 'tile')), parts along dimension 0, may hold values from 0 to 199, as said below
- res_slot: int32 [400], P('mol'), parts along dimension 0, may hold values from 0 to 199, as said below
- needed_residual_tiles: int32 [128], P(('mol', 'tile')), parts along dimension 0, may hold values from 0 to 199, as said below
- pair_energy: float32 [1536], P(('mol', 'rep')), parts along dimension 0, may hold values from -3 to -1
- virt_energy: float32 [3200], P('mol'), parts along dimension 0, may hold values from 0.2 to 3
- window_energy: float32 [16], P('mol'), parts along dimension 0, may hold values from 0.2 to 3
Outputs:
- new_amplitudes: float32 [400, 64, 768], P(('mol', 'tile'), None, 'rep'), parts along dimension 0
The draws below stay inside these ranges and needn't reach their ends.
There are 2 independent parts, one for each index of `mol`. The reference program is written for one: setup_inputs(seed, part) draws one part's arguments, and reference() takes and returns one part's arrays. A program takes and returns all parts, laid end to end along the dimension named above; each array names one. Nothing has to cross between parts.
Inputs may be any that keep to these rules, and one draw needn't show every extreme that they name: `tasks`: column k describes slot k % 512 of tile device k // 512; positions index that device's lists. `task_count`: some devices have all 512 slots live and some only 64. `amp_slot`: A permutation; slot s is stored on tile device s // 25 at position s % 25. `need_amp`: entries 8 t to 8 (t + 1) - 1 are tile device t's list: exactly 2 distinct tiles stored on each of 4 distinct owners, none on the others. `res_slot`: A permutation; slot s is owned by tile device s // 25 at position s % 25. `needed_residual_tiles`: entries 8 t to 8 (t + 1) - 1 are tile device t's list: exactly 2 distinct tiles owned by each of 4 distinct owners, none by the others.
All inputs are finite; a program needn't handle non-finite values.
Results may differ from the reference program's by a relative error of at most 0.0003.
Values sent between devices are 32-bit elements; how exact they have to be, the bound alone decides.
No kernel may reach another device: no remote copies, remote signals or barrier semaphores. Data moves between devices by JAX's collectives and lax.ppermute only.
A program may use at most 128 MiB of HBM per device.

```python
import jax
import jax.numpy as jnp
from jax import lax

NV = 1600
TW = 64
NVT = 25
ND = 8
NB = 8
CAP = 2
TASK_DEV = 512
TBLK = 64
NIJ = 768
N_TILE = 8


def to_front(values, wanted_value):
    spot = jnp.argmax(values == wanted_value).astype(jnp.int32)
    first = values[0]
    return values.at[spot].set(first).at[0].set(wanted_value)


def pick_lists(seed_key, slot_map, per_owner):
    tile_at = jnp.argsort(slot_map, stable=True).astype(jnp.int32)
    top_slot = slot_map[slot_map.shape[0] - 1]
    low_slot = slot_map[0]

    def per_device(device_key, device_id):
        head_key, tail_key = jax.random.split(device_key)
        owner_perm = jax.random.permutation(head_key, N_TILE).astype(jnp.int32)
        pinned_position = jnp.where(device_id == 0, top_slot, low_slot)
        is_forced = device_id < 2
        forced_owner = jnp.where(is_forced, pinned_position // per_owner, owner_perm[0])
        owner_perm = to_front(owner_perm, forced_owner)
        owners = owner_perm[:N_TILE // 2]
        spot_keys = jax.random.split(tail_key, N_TILE // 2)

        def choose_spots(spot_key):
            return jax.random.permutation(spot_key, per_owner).astype(jnp.int32)
        spot_perms = jax.vmap(choose_spots)(spot_keys)
        first_perm = spot_perms[0]
        forced_spot = jnp.where(is_forced, pinned_position % per_owner, first_perm[0])
        spot_perms = spot_perms.at[0].set(to_front(first_perm, forced_spot))
        positions = spot_perms[:, :CAP]
        slot_ids = owners[:, None] * per_owner + positions
        return tile_at[slot_ids.reshape(-1)]
    device_ids = jnp.arange(N_TILE, dtype=jnp.int32)
    return jax.vmap(per_device)(jax.random.split(seed_key, N_TILE), device_ids).astype(jnp.int32)


def layout(key):
    amp_tiles = ND * NVT
    res_tiles = NB * NVT
    amp_slot = jax.random.permutation(jax.random.fold_in(key, 11), amp_tiles).astype(jnp.int32)
    res_slot = jax.random.permutation(jax.random.fold_in(key, 12), res_tiles).astype(jnp.int32)
    need_amp = pick_lists(jax.random.fold_in(key, 13), amp_slot, amp_tiles // N_TILE)
    needed_residual_tiles = pick_lists(jax.random.fold_in(key, 14), res_slot, res_tiles // N_TILE)
    list_length = CAP * N_TILE // 2
    base_count = jax.random.randint(jax.random.fold_in(key, 15), (N_TILE,), TASK_DEV // 8, TASK_DEV // 2 + 1)
    is_heavy = jax.random.randint(jax.random.fold_in(key, 16), (N_TILE,), 0, 8) == 0
    counts = jnp.where(is_heavy, TASK_DEV, base_count)
    busiest = jax.random.randint(jax.random.fold_in(key, 19), (), 0, N_TILE)
    lightest = (busiest + 1 + jax.random.randint(jax.random.fold_in(key, 20), (), 0, N_TILE - 1)) % N_TILE
    device_ids = jnp.arange(N_TILE, dtype=jnp.int32)
    counts = jnp.where(device_ids == busiest, TASK_DEV, counts)
    counts = jnp.where(device_ids == lightest, TASK_DEV // 8, counts).astype(jnp.int32)
    amp_pos = jax.random.randint(jax.random.fold_in(key, 17), (N_TILE, TASK_DEV), 0, list_length)
    res_pos = jax.random.randint(jax.random.fold_in(key, 18), (N_TILE, TASK_DEV), 0, list_length)
    task_rows = jnp.stack([res_pos, amp_pos]).reshape(2, N_TILE * TASK_DEV).astype(jnp.int32)
    return (task_rows, counts, amp_slot, need_amp.reshape(-1), res_slot, needed_residual_tiles.reshape(-1))


def draw_tasks(key, part):
    return layout(key)[0]


def draw_task_count(key, part):
    return layout(key)[1]


def draw_amp_slot(key, part):
    return layout(key)[2]


def draw_need_amp(key, part):
    return layout(key)[3]


def draw_res_slot(key, part):
    return layout(key)[4]


def draw_needed_residual_tiles(key, part):
    return layout(key)[5]


def level_of(stream_key, dims, pieces, least, top_value):
    def one(position, blocks):
        steps = jax.random.uniform(jax.random.fold_in(jax.random.fold_in(stream_key, 6), position), (blocks,), jnp.float32, least / len(pieces), top_value / len(pieces))
        return jnp.repeat(jnp.exp(steps), dims[position] // blocks).reshape((-1,) + (1,) * (len(dims) - position - 1))

    gain = one(*pieces[0])
    for cut in pieces[1:]:
        gain = gain * one(*cut)
    return gain


def bell_draw(stream_key, extent, deviation, limit, cuts=(), held_as=jnp.bfloat16):
    result = deviation * jax.random.normal(stream_key, extent, jnp.float32)
    if cuts:
        result = result * level_of(stream_key, extent, cuts, -0.22, 0.18)
    return jnp.clip(result, -limit, limit).astype(held_as)


def setup_inputs(seed: int = 0, part: int = 0) -> dict:
    seeds = jax.random.split(jax.random.key(seed), 12)
    part_keys = jax.random.split(jax.random.fold_in(seeds[11], part), 12)
    tasks = draw_tasks(jax.random.fold_in(jax.random.fold_in(seeds[11], part), 71), part)
    task_count = draw_task_count(jax.random.fold_in(jax.random.fold_in(seeds[11], part), 71), part)
    integrals = bell_draw(part_keys[2], (N_TILE * TASK_DEV, TW * TW), (TW * 16) ** -0.5, 0.1875, ((0, 8),), jnp.float32)
    amplitudes = bell_draw(part_keys[3], (ND * NVT, TW, NIJ), 1.0, 6.0, ((0, 8), (2, 2)), jnp.float32)
    amp_slot = draw_amp_slot(jax.random.fold_in(jax.random.fold_in(seeds[11], part), 71), part)
    need_amp = draw_need_amp(jax.random.fold_in(jax.random.fold_in(seeds[11], part), 71), part)
    res_slot = draw_res_slot(jax.random.fold_in(jax.random.fold_in(seeds[11], part), 71), part)
    needed_residual_tiles = draw_needed_residual_tiles(jax.random.fold_in(jax.random.fold_in(seeds[11], part), 71), part)
    pair_energy = jnp.clip(-3.0 + 2.0 * jax.random.uniform(part_keys[8], (NIJ,), jnp.float32) ** level_of(part_keys[8], (NIJ,), ((0, 2),), -0.2, 0.2), -3.0, -1.0)
    virt_energy = jnp.clip(jax.random.uniform(part_keys[9], (NV,), jnp.float32, 0.2, 3.0), 0.2, 3.0)
    window_energy = jnp.clip(jax.random.uniform(part_keys[10], (NB,), jnp.float32, 0.2, 3.0), 0.2, 3.0)
    return dict(tasks=tasks, task_count=task_count, integrals=integrals, amplitudes=amplitudes, amp_slot=amp_slot, need_amp=need_amp, res_slot=res_slot, needed_residual_tiles=needed_residual_tiles, pair_energy=pair_energy, virt_energy=virt_energy, window_energy=window_energy)


def reference(tasks, task_count, integrals, amplitudes, amp_slot, need_amp, res_slot, needed_residual_tiles, pair_energy, virt_energy, window_energy):
    all_tasks = tasks.shape[1]
    per_device = all_tasks // N_TILE
    counter = jnp.arange(all_tasks, dtype=jnp.int32)
    owner_of = counter // per_device
    within = counter % per_device
    is_live = within < task_count[owner_of]
    list_length = need_amp.shape[0] // N_TILE
    amp_tile = need_amp[owner_of * list_length + tasks[1]]
    residual_block = needed_residual_tiles[owner_of * list_length + tasks[0]]
    amp_position = amp_slot[amp_tile]
    res_count = NB * NVT

    def cut_rows(values, block_index):
        return lax.dynamic_slice_in_dim(values, (block_index * TBLK).astype(jnp.int32), TBLK, 0)

    def contract(totals, block_index):
        operator_matrices = cut_rows(integrals, block_index).reshape(TBLK, TW, TW)
        input_factor = amplitudes[cut_rows(amp_position, block_index)]
        contracted_output = jnp.einsum('fzo,fou->fzu', operator_matrices, input_factor, precision=lax.Precision.HIGHEST)
        contracted_output = jnp.where(cut_rows(is_live, block_index)[:, None, None], contracted_output, jnp.zeros_like(contracted_output))
        return totals.at[cut_rows(residual_block, block_index)].add(contracted_output), None

    start_totals = jnp.zeros((res_count, TW, NIJ), jnp.float32)
    summed, _ = lax.scan(contract, start_totals, jnp.arange(all_tasks // TBLK, dtype=jnp.int32))
    tile_ids = jnp.arange(res_count, dtype=jnp.int32)
    column = tile_ids % NVT
    window = tile_ids // NVT
    virt_part = virt_energy.reshape(NVT, TW)[column]
    window_part = window_energy[window]
    denominator = pair_energy[None, None, :] - virt_part[:, :, None] - window_part[:, None, None]
    return jnp.zeros_like(summed).at[res_slot].set(summed / denominator)
```

```python
import functools

import jax
import jax.numpy as jnp
from jax import lax
from jax.experimental import pallas as pl
from jax.experimental.pallas import tpu as pltpu
from jax.sharding import PartitionSpec as P

TW = 64
CAP = 2
VMEM_LIMIT = 56 * 1024 * 1024
F32 = jnp.float32
BF16 = jnp.bfloat16

HBM_SPEC = pl.BlockSpec(memory_space=pl.ANY)
SMEM_SPEC = pl.BlockSpec(memory_space=pltpu.SMEM)
VMEM_SPEC = pl.BlockSpec(memory_space=pltpu.VMEM)


def params(limit=VMEM_LIMIT):
    return pltpu.CompilerParams(vmem_limit_bytes=limit)


def cost(flops, touched):
    return pl.CostEstimate(flops=flops, bytes_accessed=touched, transcendentals=0)


def clear(ref, count, value):
    @pl.loop(0, count)
    def _(i):
        ref[i] = value


def pack_kernel(owners, per_owner, width, me_ref, lists_ref, amp_slot_ref, amplitudes, *rest):
    outs, picked, seen, sems = rest[: owners - 1], rest[-3], rest[-2], rest[-1]
    list_length = lists_ref.shape[0] // owners // 2
    start = width[0]
    me = me_ref[0]
    low = me * per_owner
    clear(picked, owners * CAP, -1)
    clear(seen, owners, 0)

    @pl.loop(0, owners * list_length)
    def _(i):
        partner = i // list_length
        tile = lists_ref[partner * 2 * list_length + i % list_length]
        local = amp_slot_ref[tile] - low
        mine = (local >= 0) & (local < per_owner)

        @pl.when(mine)
        def _():
            count = seen[partner]
            picked[partner * CAP + count] = local
            seen[partner] = count + 1

    def copy(d, k):
        partner = jnp.bitwise_xor(me, d)
        local = picked[partner * CAP + k]
        return local, pltpu.make_async_copy(
            amplitudes.at[jnp.maximum(local, 0), :, pl.ds(start, width[1])],
            outs[d - 1].at[k],
            sems.at[d * CAP + k],
        )

    for step in ("start", "wait"):
        for d in range(owners - 1, 0, -1):
            for k in range(CAP):
                local, moved = copy(d, k)
                pl.when(local >= 0)(getattr(moved, step))


def maps_kernel(
    owners, per_amp, per_res, me_ref, lists_ref, amp_slot_ref, res_slot_ref,
    amp_from, amp_self, res_to, res_from, res_tile, seen,
):
    list_length = lists_ref.shape[0] // owners // 2
    me = me_ref[0]
    for ref in (amp_from, res_to, res_from):
        clear(ref, owners * CAP, -1)
    clear(amp_self, CAP, 0)
    clear(res_tile, owners * CAP, 0)

    def own_list(offset, slot_map, per_owner, place):
        clear(seen, owners, 0)

        @pl.loop(0, list_length)
        def _(g):
            slot = slot_map[lists_ref[me * 2 * list_length + offset + g]]
            owner = slot // per_owner
            d = jnp.bitwise_xor(owner, me)
            count = seen[d]
            place(d * CAP + count, g, slot - owner * per_owner, d, count)
            seen[d] = count + 1

    def place_amp(at, g, local, d, count):
        amp_from[at] = g

        @pl.when(d == 0)
        def _():
            amp_self[count] = local

    def place_res(at, g, local, d, count):
        res_to[at] = g

    own_list(0, amp_slot_ref, per_amp, place_amp)
    own_list(list_length, res_slot_ref, per_res, place_res)
    clear(seen, owners, 0)
    low = me * per_res

    @pl.loop(0, owners * list_length)
    def _(i):
        partner = i // list_length
        tile = lists_ref[partner * 2 * list_length + list_length + i % list_length]
        local = res_slot_ref[tile] - low

        @pl.when((local >= 0) & (local < per_res))
        def _():
            d = jnp.bitwise_xor(partner, me)
            count = seen[d]
            res_from[d * CAP + count] = local
            res_tile[d * CAP + count] = tile
            seen[d] = count + 1


def sum_kernel(count_ref, tasks_ref, integrals_ref, sums_ref, hits):
    slots = sums_ref.shape[0]
    tasks_here = integrals_ref.shape[0]
    list_length = int(round(slots**0.5))

    @pl.when(pl.program_id(0) == 0)
    def _():
        pair = tasks_ref[0:1, :] * list_length + tasks_ref[1:2, :]
        spot = lax.broadcasted_iota(jnp.int32, (1, tasks_here), 1)
        pair = jnp.where(spot < count_ref[0], pair, -1)
        row = lax.broadcasted_iota(jnp.int32, (slots, tasks_here), 0)
        hits[...] = jnp.where(row == pair, 1.0, 0.0).astype(BF16)

    rows = integrals_ref[...]
    high = rows.astype(BF16)
    low = (rows - high.astype(F32)).astype(BF16)
    sums_ref[...] = jnp.dot(hits[...], high, preferred_element_type=F32) + jnp.dot(
        hits[...], low, preferred_element_type=F32
    )


def product_kernel(owners, width, amp_from, amp_self, res_to, operator, amplitudes, *rest):
    arrived, outs = rest[: owners - 1], rest[owners - 1 : 2 * owners - 1]
    table, high, low, totals, in_sems, out_sems = rest[2 * owners - 1 :]
    start, columns = width
    rows = operator.shape[0]

    def fetch(d, k):
        g = amp_from[d * CAP + k]
        if d == 0:
            source = amplitudes.at[amp_self[k], :, pl.ds(start, columns)]
        else:
            source = arrived[d - 1].at[k]
        return g, pltpu.make_async_copy(source, table.at[jnp.maximum(g, 0)], in_sems.at[d * CAP + k])

    def deliver(d, k):
        g = res_to[d * CAP + k]
        return g, pltpu.make_async_copy(totals.at[jnp.maximum(g, 0)], outs[d].at[k], out_sems.at[d * CAP + k])

    def each(move, step):
        for d in range(owners):
            for k in range(CAP):
                g, moved = move(d, k)
                pl.when(g >= 0)(getattr(moved, step))

    each(fetch, "start")
    each(fetch, "wait")
    values = table[...].reshape(rows, columns)
    top = values.astype(BF16)
    high[...] = top
    low[...] = (values - top.astype(F32)).astype(BF16)
    step = 2 * TW

    @pl.loop(0, rows // step)
    def _(i):
        left = operator[pl.ds(pl.multiple_of(i * step, step), step), :]
        left_high = left.astype(BF16)
        left_low = (left - left_high.astype(F32)).astype(BF16)
        total = jnp.dot(left_high, low[...], preferred_element_type=F32)
        total += jnp.dot(left_low, high[...], preferred_element_type=F32)
        total += jnp.dot(left_high, high[...], preferred_element_type=F32)
        totals[pl.ds(i * 2, 2)] = total.reshape(2, TW, columns)

    each(deliver, "start")
    each(deliver, "wait")


def final_kernel(owners, width, tiles, chained, res_from, res_tile, window, pair, virt, *rest):
    arrived, (out, table, sums, in_sems, out_sem) = rest[:owners], rest[-5:]
    start, columns = width
    per_res = sums.shape[0]

    def fetch(d, k):
        local = res_from[d * CAP + k]
        return local, pltpu.make_async_copy(arrived[d].at[k], table.at[d * CAP + k], in_sems.at[d * CAP + k])

    for d in range(owners):
        for k in range(CAP):
            local, moved = fetch(d, k)
            pl.when(local >= 0)(moved.start)

    sums[...] = jnp.zeros_like(sums)
    for d in range(owners):
        for k in range(CAP):
            local, moved = fetch(d, k)

            @pl.when(local >= 0)
            def _():
                moved.wait()
                tile = res_tile[d * CAP + k]
                column = tile % tiles
                base = pair[...] - window[tile // tiles]
                below = base - jnp.concatenate([virt[column]] * (columns // 128), axis=1)
                sums[local] = sums[local] + table[d * CAP + k] / below

    written = pltpu.make_async_copy(sums, out.at[:, :, pl.ds(start, columns)], out_sem)
    written.start()
    written.wait()


def local(
    tasks,
    task_count,
    integrals,
    amplitudes,
    amp_slot,
    need_amp,
    res_slot,
    needed_residual_tiles,
    pair_energy,
    virt_energy,
    window_energy,
):
    owners = lax.axis_size("tile")
    me = lax.axis_index("tile").astype(jnp.int32)
    per_amp, _, row_count = amplitudes.shape
    per_res = res_slot.shape[0] // owners
    list_length = need_amp.shape[0]
    tile_count = virt_energy.shape[0] // TW
    slots = list_length * list_length
    task_slots = tasks.shape[1]
    chunks = [(0, row_count)]

    own_lists = jnp.concatenate([need_amp, needed_residual_tiles])
    spots = jnp.arange(owners, dtype=jnp.int32)[:, None] == me
    lists = lax.psum(jnp.where(spots, own_lists[None, :], 0), "tile").reshape(-1)
    me_ref = me.reshape(1)

    def exchange(buffers):
        return [
            lax.ppermute(buffers[d - 1], "tile", [(i, i ^ d) for i in range(owners)])
            for d in range(1, owners)
        ]

    def pack(chunk):
        piece = jax.ShapeDtypeStruct((CAP, TW, chunk[1]), F32)
        return pl.pallas_call(
            functools.partial(pack_kernel, owners, per_amp, chunk),
            out_shape=[piece] * (owners - 1),
            in_specs=[SMEM_SPEC] * 3 + [HBM_SPEC],
            out_specs=[HBM_SPEC] * (owners - 1),
            scratch_shapes=[
                pltpu.SMEM((owners * CAP,), jnp.int32),
                pltpu.SMEM((owners,), jnp.int32),
                pltpu.SemaphoreType.DMA((owners * CAP,)),
            ],
            compiler_params=params(),
            cost_estimate=cost(0, 2 * list_length * TW * chunk[1] * 4),
            name="pack_tiles",
        )(me_ref, lists, amp_slot, amplitudes)

    fetched = [exchange(pack(chunk)) for chunk in chunks]

    small = jax.ShapeDtypeStruct((owners * CAP,), jnp.int32)
    amp_from, amp_self, res_to, res_from, res_tile = pl.pallas_call(
        functools.partial(maps_kernel, owners, per_amp, per_res),
        out_shape=[small, jax.ShapeDtypeStruct((CAP,), jnp.int32), small, small, small],
        in_specs=[SMEM_SPEC] * 4,
        out_specs=[SMEM_SPEC] * 5,
        scratch_shapes=[pltpu.SMEM((owners,), jnp.int32)],
        compiler_params=params(),
        name="list_maps",
    )(me_ref, lists, amp_slot, res_slot)

    block = 512
    sums = pl.pallas_call(
        sum_kernel,
        grid=(TW * TW // block,),
        out_shape=jax.ShapeDtypeStruct((slots, TW * TW), F32),
        in_specs=[
            SMEM_SPEC,
            pl.BlockSpec((2, task_slots), lambda i: (0, 0)),
            pl.BlockSpec((task_slots, block), lambda i: (0, i)),
        ],
        out_specs=pl.BlockSpec((slots, block), lambda i: (0, i)),
        scratch_shapes=[pltpu.VMEM((slots, task_slots), BF16)],
        compiler_params=params(),
        cost_estimate=cost(4 * slots * task_slots * TW * TW, (task_slots + slots) * TW * TW * 4),
        name="sum_integrals",
    )(task_count, tasks, integrals)
    operator = (
        sums.reshape(list_length, list_length, TW, TW)
        .transpose(0, 2, 1, 3)
        .reshape(list_length * TW, list_length * TW)
    )

    def multiply(chunk, pieces):
        depth = list_length * TW
        piece = jax.ShapeDtypeStruct((CAP, TW, chunk[1]), F32)
        return pl.pallas_call(
            functools.partial(product_kernel, owners, chunk),
            out_shape=[piece] * owners,
            in_specs=[SMEM_SPEC] * 3 + [VMEM_SPEC] + [HBM_SPEC] * owners,
            out_specs=[HBM_SPEC] * owners,
            scratch_shapes=[
                pltpu.VMEM((list_length, TW, chunk[1]), F32),
                pltpu.VMEM((depth, chunk[1]), BF16),
                pltpu.VMEM((depth, chunk[1]), BF16),
                pltpu.VMEM((list_length, TW, chunk[1]), F32),
                pltpu.SemaphoreType.DMA((owners * CAP,)),
                pltpu.SemaphoreType.DMA((owners * CAP,)),
            ],
            compiler_params=params(),
            cost_estimate=cost(6 * depth * depth * chunk[1], 4 * depth * (depth + 2 * chunk[1])),
            name="multiply_tiles",
        )(amp_from, amp_self, res_to, operator, amplitudes, *pieces)

    virt = jnp.broadcast_to(virt_energy.reshape(tile_count, TW, 1), (tile_count, TW, 128))
    pair = pair_energy.reshape(1, row_count)

    def finish(chunk, pieces):
        return pl.pallas_call(
            functools.partial(final_kernel, owners, chunk, tile_count, False),
            out_shape=jax.ShapeDtypeStruct((per_res, TW, row_count), F32),
            in_specs=[SMEM_SPEC] * 3 + [VMEM_SPEC] * 2 + [HBM_SPEC] * owners,
            out_specs=HBM_SPEC,
            scratch_shapes=[
                pltpu.VMEM((owners * CAP, TW, chunk[1]), F32),
                pltpu.VMEM((per_res, TW, chunk[1]), F32),
                pltpu.SemaphoreType.DMA((owners * CAP,)),
                pltpu.SemaphoreType.DMA,
            ],
            compiler_params=params(),
            cost_estimate=cost(0, per_res * TW * chunk[1] * 4),
            name="finish_tiles",
        )(res_from, res_tile, window_energy, pair, virt, *pieces)

    for chunk, pieces in zip(chunks, fetched):
        products = multiply(chunk, pieces)
        result = finish(chunk, [products[0]] + exchange(products[1:]))
    return result


def solution(mesh):
    in_specs = (
        P(None, ("mol", "tile")),
        P(("mol", "tile")),
        P(("mol", "tile"), None),
        P(("mol", "tile"), None, "rep"),
        P("mol"),
        P(("mol", "tile")),
        P("mol"),
        P(("mol", "tile")),
        P(("mol", "rep")),
        P("mol"),
        P("mol"),
    )
    out_specs = P(("mol", "tile"), None, "rep")
    return jax.shard_map(local, mesh=mesh, in_specs=in_specs, out_specs=out_specs, check_vma=False)
```

```python
import functools

import jax
import jax.numpy as jnp
from jax import lax
from jax.experimental import pallas as pl
from jax.experimental.pallas import tpu as pltpu
from jax.sharding import PartitionSpec as P

TW = 64
CAP = 2
VMEM_LIMIT = 56 * 1024 * 1024
F32 = jnp.float32
BF16 = jnp.bfloat16

HBM_SPEC = pl.BlockSpec(memory_space=pl.ANY)
SMEM_SPEC = pl.BlockSpec(memory_space=pltpu.SMEM)
VMEM_SPEC = pl.BlockSpec(memory_space=pltpu.VMEM)


def params(limit=VMEM_LIMIT):
    return pltpu.CompilerParams(vmem_limit_bytes=limit)


def cost(flops, touched):
    return pl.CostEstimate(flops=flops, bytes_accessed=touched, transcendentals=0)


def clear(ref, count, value):
    @pl.loop(0, count)
    def _(i):
        ref[i] = value


def pack_kernel(owners, per_owner, width, me_ref, lists_ref, amp_slot_ref, amplitudes, *rest):
    outs, (staged, picked, seen, in_sems, out_sems) = rest[: owners - 1], rest[-5:]
    list_length = lists_ref.shape[0] // owners // 2
    start = width[0]
    me = me_ref[0]
    low = me * per_owner
    clear(picked, owners * CAP, -1)
    clear(seen, owners, 0)

    @pl.loop(0, owners * list_length)
    def _(i):
        partner = i // list_length
        tile = lists_ref[partner * 2 * list_length + i % list_length]
        local = amp_slot_ref[tile] - low
        mine = (local >= 0) & (local < per_owner)

        @pl.when(mine)
        def _():
            count = seen[partner]
            picked[partner * CAP + count] = local
            seen[partner] = count + 1

    def load(d, k):
        spot = d * CAP + k
        local = picked[jnp.bitwise_xor(me, d) * CAP + k]
        source = amplitudes.at[jnp.maximum(local, 0), :, pl.ds(start, width[1])]
        return local, pltpu.make_async_copy(source, staged.at[spot], in_sems.at[spot])

    def store(d, k):
        spot = d * CAP + k
        local = picked[jnp.bitwise_xor(me, d) * CAP + k]
        return local, pltpu.make_async_copy(staged.at[spot], outs[d - 1].at[k], out_sems.at[spot])

    spots = [(d, k) for d in range(owners - 1, 0, -1) for k in range(CAP)]
    for d, k in spots:
        local, loaded = load(d, k)
        pl.when(local >= 0)(loaded.start)
    for d, k in spots:
        local, loaded = load(d, k)
        _, stored = store(d, k)

        @pl.when(local >= 0)
        def _():
            loaded.wait()
            stored.start()

    for d, k in spots:
        local, stored = store(d, k)
        pl.when(local >= 0)(stored.wait)


def maps_kernel(
    owners, per_amp, per_res, me_ref, lists_ref, amp_slot_ref, res_slot_ref,
    amp_from, amp_self, res_to, res_from, res_tile, seen,
):
    list_length = lists_ref.shape[0] // owners // 2
    me = me_ref[0]
    for ref in (amp_from, res_to, res_from):
        clear(ref, owners * CAP, -1)
    clear(amp_self, CAP, 0)
    clear(res_tile, owners * CAP, 0)

    def own_list(offset, slot_map, per_owner, place):
        clear(seen, owners, 0)

        @pl.loop(0, list_length)
        def _(g):
            slot = slot_map[lists_ref[me * 2 * list_length + offset + g]]
            owner = slot // per_owner
            d = jnp.bitwise_xor(owner, me)
            count = seen[d]
            place(d * CAP + count, g, slot - owner * per_owner, d, count)
            seen[d] = count + 1

    def place_amp(at, g, local, d, count):
        amp_from[at] = g

        @pl.when(d == 0)
        def _():
            amp_self[count] = local

    def place_res(at, g, local, d, count):
        res_to[at] = g

    own_list(0, amp_slot_ref, per_amp, place_amp)
    own_list(list_length, res_slot_ref, per_res, place_res)
    clear(seen, owners, 0)
    low = me * per_res

    @pl.loop(0, owners * list_length)
    def _(i):
        partner = i // list_length
        tile = lists_ref[partner * 2 * list_length + list_length + i % list_length]
        local = res_slot_ref[tile] - low

        @pl.when((local >= 0) & (local < per_res))
        def _():
            d = jnp.bitwise_xor(partner, me)
            count = seen[d]
            res_from[d * CAP + count] = local
            res_tile[d * CAP + count] = tile
            seen[d] = count + 1


def sum_kernel(count_ref, tasks_ref, integrals_ref, sums_ref, hits):
    slots = sums_ref.shape[0]
    tasks_here = integrals_ref.shape[0]
    list_length = int(round(slots**0.5))

    @pl.when(pl.program_id(0) == 0)
    def _():
        pair = tasks_ref[0:1, :] * list_length + tasks_ref[1:2, :]
        spot = lax.broadcasted_iota(jnp.int32, (1, tasks_here), 1)
        pair = jnp.where(spot < count_ref[0], pair, -1)
        row = lax.broadcasted_iota(jnp.int32, (slots, tasks_here), 0)
        hits[...] = jnp.where(row == pair, 1.0, 0.0).astype(BF16)

    rows = integrals_ref[...]
    high = rows.astype(BF16)
    low = (rows - high.astype(F32)).astype(BF16)
    sums_ref[...] = jnp.dot(hits[...], high, preferred_element_type=F32) + jnp.dot(
        hits[...], low, preferred_element_type=F32
    )


def product_kernel(owners, width, amp_from, amp_self, res_to, operator, amplitudes, *rest):
    arrived, outs = rest[: owners - 1], rest[owners - 1 : 2 * owners - 1]
    table, high, low, totals, in_sems, out_sems = rest[2 * owners - 1 :]
    start, columns = width
    rows = operator.shape[0]

    def fetch(d, k):
        g = amp_from[d * CAP + k]
        if d == 0:
            source = amplitudes.at[amp_self[k], :, pl.ds(start, columns)]
        else:
            source = arrived[d - 1].at[k]
        return g, pltpu.make_async_copy(source, table.at[jnp.maximum(g, 0)], in_sems.at[d * CAP + k])

    def deliver(d, k):
        g = res_to[d * CAP + k]
        return g, pltpu.make_async_copy(totals.at[jnp.maximum(g, 0)], outs[d].at[k], out_sems.at[d * CAP + k])

    def each(move, step):
        for d in range(owners):
            for k in range(CAP):
                g, moved = move(d, k)
                pl.when(g >= 0)(getattr(moved, step))

    each(fetch, "start")
    each(fetch, "wait")
    values = table[...].reshape(rows, columns)
    top = values.astype(BF16)
    high[...] = top
    low[...] = (values - top.astype(F32)).astype(BF16)
    step = 2 * TW

    @pl.loop(0, rows // step)
    def _(i):
        left = operator[pl.ds(pl.multiple_of(i * step, step), step), :]
        left_high = left.astype(BF16)
        left_low = (left - left_high.astype(F32)).astype(BF16)
        total = jnp.dot(left_high, low[...], preferred_element_type=F32)
        total += jnp.dot(left_low, high[...], preferred_element_type=F32)
        total += jnp.dot(left_high, high[...], preferred_element_type=F32)
        totals[pl.ds(i * 2, 2)] = total.reshape(2, TW, columns)

    each(deliver, "start")
    each(deliver, "wait")


def final_kernel(owners, width, tiles, chained, res_from, res_tile, window, pair, virt, *rest):
    arrived, (out, table, sums, in_sems, out_sem) = rest[:owners], rest[-5:]
    start, columns = width
    per_res = sums.shape[0]

    def fetch(d, k):
        local = res_from[d * CAP + k]
        return local, pltpu.make_async_copy(arrived[d].at[k], table.at[d * CAP + k], in_sems.at[d * CAP + k])

    for d in range(owners):
        for k in range(CAP):
            local, moved = fetch(d, k)
            pl.when(local >= 0)(moved.start)

    sums[...] = jnp.zeros_like(sums)
    for d in range(owners):
        for k in range(CAP):
            local, moved = fetch(d, k)

            @pl.when(local >= 0)
            def _():
                moved.wait()
                tile = res_tile[d * CAP + k]
                column = tile % tiles
                base = pair[...] - window[tile // tiles]
                below = base - jnp.concatenate([virt[column]] * (columns // 128), axis=1)
                sums[local] = sums[local] + table[d * CAP + k] / below

    written = pltpu.make_async_copy(sums, out.at[:, :, pl.ds(start, columns)], out_sem)
    written.start()
    written.wait()


def local(
    tasks,
    task_count,
    integrals,
    amplitudes,
    amp_slot,
    need_amp,
    res_slot,
    needed_residual_tiles,
    pair_energy,
    virt_energy,
    window_energy,
):
    owners = lax.axis_size("tile")
    me = lax.axis_index("tile").astype(jnp.int32)
    per_amp, _, row_count = amplitudes.shape
    per_res = res_slot.shape[0] // owners
    list_length = need_amp.shape[0]
    tile_count = virt_energy.shape[0] // TW
    slots = list_length * list_length
    task_slots = tasks.shape[1]
    chunks = [(0, row_count)]

    own_lists = jnp.concatenate([need_amp, needed_residual_tiles])
    spots = jnp.arange(owners, dtype=jnp.int32)[:, None] == me
    lists = lax.psum(jnp.where(spots, own_lists[None, :], 0), "tile").reshape(-1)
    me_ref = me.reshape(1)

    def exchange(buffers):
        return [
            lax.ppermute(buffers[d - 1], "tile", [(i, i ^ d) for i in range(owners)])
            for d in range(1, owners)
        ]

    def pack(chunk):
        piece = jax.ShapeDtypeStruct((CAP, TW, chunk[1]), F32)
        return pl.pallas_call(
            functools.partial(pack_kernel, owners, per_amp, chunk),
            out_shape=[piece] * (owners - 1),
            in_specs=[SMEM_SPEC] * 3 + [HBM_SPEC],
            out_specs=[HBM_SPEC] * (owners - 1),
            scratch_shapes=[
                pltpu.VMEM((owners * CAP, TW, chunk[1]), F32),
                pltpu.SMEM((owners * CAP,), jnp.int32),
                pltpu.SMEM((owners,), jnp.int32),
                pltpu.SemaphoreType.DMA((owners * CAP,)),
                pltpu.SemaphoreType.DMA((owners * CAP,)),
            ],
            compiler_params=params(),
            cost_estimate=cost(0, 2 * list_length * TW * chunk[1] * 4),
            name="pack_tiles",
        )(me_ref, lists, amp_slot, amplitudes)

    fetched = [exchange(pack(chunk)) for chunk in chunks]

    small = jax.ShapeDtypeStruct((owners * CAP,), jnp.int32)
    amp_from, amp_self, res_to, res_from, res_tile = pl.pallas_call(
        functools.partial(maps_kernel, owners, per_amp, per_res),
        out_shape=[small, jax.ShapeDtypeStruct((CAP,), jnp.int32), small, small, small],
        in_specs=[SMEM_SPEC] * 4,
        out_specs=[SMEM_SPEC] * 5,
        scratch_shapes=[pltpu.SMEM((owners,), jnp.int32)],
        compiler_params=params(),
        name="list_maps",
    )(me_ref, lists, amp_slot, res_slot)

    block = 512
    sums = pl.pallas_call(
        sum_kernel,
        grid=(TW * TW // block,),
        out_shape=jax.ShapeDtypeStruct((slots, TW * TW), F32),
        in_specs=[
            SMEM_SPEC,
            pl.BlockSpec((2, task_slots), lambda i: (0, 0)),
            pl.BlockSpec((task_slots, block), lambda i: (0, i)),
        ],
        out_specs=pl.BlockSpec((slots, block), lambda i: (0, i)),
        scratch_shapes=[pltpu.VMEM((slots, task_slots), BF16)],
        compiler_params=params(),
        cost_estimate=cost(4 * slots * task_slots * TW * TW, (task_slots + slots) * TW * TW * 4),
        name="sum_integrals",
    )(task_count, tasks, integrals)
    operator = (
        sums.reshape(list_length, list_length, TW, TW)
        .transpose(0, 2, 1, 3)
        .reshape(list_length * TW, list_length * TW)
    )

    def multiply(chunk, pieces):
        depth = list_length * TW
        piece = jax.ShapeDtypeStruct((CAP, TW, chunk[1]), F32)
        return pl.pallas_call(
            functools.partial(product_kernel, owners, chunk),
            out_shape=[piece] * owners,
            in_specs=[SMEM_SPEC] * 3 + [VMEM_SPEC] + [HBM_SPEC] * owners,
            out_specs=[HBM_SPEC] * owners,
            scratch_shapes=[
                pltpu.VMEM((list_length, TW, chunk[1]), F32),
                pltpu.VMEM((depth, chunk[1]), BF16),
                pltpu.VMEM((depth, chunk[1]), BF16),
                pltpu.VMEM((list_length, TW, chunk[1]), F32),
                pltpu.SemaphoreType.DMA((owners * CAP,)),
                pltpu.SemaphoreType.DMA((owners * CAP,)),
            ],
            compiler_params=params(),
            cost_estimate=cost(6 * depth * depth * chunk[1], 4 * depth * (depth + 2 * chunk[1])),
            name="multiply_tiles",
        )(amp_from, amp_self, res_to, operator, amplitudes, *pieces)

    virt = jnp.broadcast_to(virt_energy.reshape(tile_count, TW, 1), (tile_count, TW, 128))
    pair = pair_energy.reshape(1, row_count)

    def finish(chunk, pieces):
        return pl.pallas_call(
            functools.partial(final_kernel, owners, chunk, tile_count, False),
            out_shape=jax.ShapeDtypeStruct((per_res, TW, row_count), F32),
            in_specs=[SMEM_SPEC] * 3 + [VMEM_SPEC] * 2 + [HBM_SPEC] * owners,
            out_specs=HBM_SPEC,
            scratch_shapes=[
                pltpu.VMEM((owners * CAP, TW, chunk[1]), F32),
                pltpu.VMEM((per_res, TW, chunk[1]), F32),
                pltpu.SemaphoreType.DMA((owners * CAP,)),
                pltpu.SemaphoreType.DMA,
            ],
            compiler_params=params(),
            cost_estimate=cost(0, per_res * TW * chunk[1] * 4),
            name="finish_tiles",
        )(res_from, res_tile, window_energy, pair, virt, *pieces)

    for chunk, pieces in zip(chunks, fetched):
        products = multiply(chunk, pieces)
        result = finish(chunk, [products[0]] + exchange(products[1:]))
    return result


def solution(mesh):
    in_specs = (
        P(None, ("mol", "tile")),
        P(("mol", "tile")),
        P(("mol", "tile"), None),
        P(("mol", "tile"), None, "rep"),
        P("mol"),
        P(("mol", "tile")),
        P("mol"),
        P(("mol", "tile")),
        P(("mol", "rep")),
        P("mol"),
        P("mol"),
    )
    out_specs = P(("mol", "tile"), None, "rep")
    return jax.shard_map(local, mesh=mesh, in_specs=in_specs, out_specs=out_specs, check_vma=False)
```

```python
import functools

import jax
import jax.numpy as jnp
from jax import lax
from jax.experimental import pallas as pl
from jax.experimental.pallas import tpu as pltpu
from jax.sharding import PartitionSpec as P

TW = 64
CAP = 2
VMEM_LIMIT = 56 * 1024 * 1024
F32 = jnp.float32
BF16 = jnp.bfloat16

HBM_SPEC = pl.BlockSpec(memory_space=pl.ANY)
SMEM_SPEC = pl.BlockSpec(memory_space=pltpu.SMEM)
VMEM_SPEC = pl.BlockSpec(memory_space=pltpu.VMEM)


def params(limit=VMEM_LIMIT):
    return pltpu.CompilerParams(vmem_limit_bytes=limit)


def cost(flops, touched):
    return pl.CostEstimate(flops=flops, bytes_accessed=touched, transcendentals=0)


def clear(ref, count, value):
    @pl.loop(0, count)
    def _(i):
        ref[i] = value


def pack_kernel(owners, per_owner, me_ref, lists_ref, amp_slot_ref, amplitudes, *rest):
    outs, (picked, sems) = rest[: owners - 1], rest[-2:]
    list_length = lists_ref.shape[0] // owners // 2
    me = me_ref[0]
    low = me * per_owner
    clear(picked, owners * CAP, -1)

    @pl.loop(0, owners)
    def _(partner):
        def note(j, count):
            local = amp_slot_ref[lists_ref[partner * 2 * list_length + j]] - low
            mine = (local >= 0) & (local < per_owner)
            picked[jnp.where(mine, partner * CAP + count, owners * CAP)] = local
            return count + mine.astype(jnp.int32)

        lax.fori_loop(0, list_length, note, jnp.int32(0), unroll=8)

    for step in ("start", "wait"):
        for d in range(owners - 1, 0, -1):
            for k in range(CAP):
                local = picked[jnp.bitwise_xor(me, d) * CAP + k]
                moved = pltpu.make_async_copy(
                    amplitudes.at[jnp.maximum(local, 0)], outs[d - 1].at[k], sems.at[d * CAP + k]
                )
                pl.when(local >= 0)(getattr(moved, step))


def maps_kernel(
    owners, per_amp, per_res, me_ref, lists_ref, amp_slot_ref, res_slot_ref,
    amp_from, amp_self, res_to, res_from, res_tile, res_first, seen, taken,
):
    list_length = lists_ref.shape[0] // owners // 2
    me = me_ref[0]
    for ref in (amp_from, res_to, res_from):
        clear(ref, owners * CAP, -1)
    clear(amp_self, CAP, 0)
    clear(res_tile, owners * CAP, 0)
    clear(res_first, owners * CAP, -1)
    clear(taken, per_res, -1)

    def own_list(offset, slot_map, per_owner, place):
        clear(seen, owners, 0)

        @pl.loop(0, list_length)
        def _(g):
            slot = slot_map[lists_ref[me * 2 * list_length + offset + g]]
            owner = slot // per_owner
            d = jnp.bitwise_xor(owner, me)
            count = seen[d]
            place(d * CAP + count, g, slot - owner * per_owner, d, count)
            seen[d] = count + 1

    def place_amp(at, g, local, d, count):
        amp_from[at] = g

        @pl.when(d == 0)
        def _():
            amp_self[count] = local

    def place_res(at, g, local, d, count):
        res_to[at] = g

    own_list(0, amp_slot_ref, per_amp, place_amp)
    own_list(list_length, res_slot_ref, per_res, place_res)
    clear(seen, owners, 0)
    low = me * per_res

    @pl.loop(0, owners * list_length)
    def _(i):
        partner = i // list_length
        tile = lists_ref[partner * 2 * list_length + list_length + i % list_length]
        local = res_slot_ref[tile] - low

        @pl.when((local >= 0) & (local < per_res))
        def _():
            d = jnp.bitwise_xor(partner, me)
            count = seen[d]
            res_from[d * CAP + count] = local
            res_tile[d * CAP + count] = tile
            seen[d] = count + 1

    @pl.loop(0, owners * CAP)
    def _(spot):
        local = res_from[spot]

        @pl.when(local >= 0)
        def _():
            @pl.when(taken[local] < 0)
            def _():
                taken[local] = spot

            res_first[spot] = taken[local]


def sum_kernel(count_ref, tasks_ref, integrals_ref, sums_ref, blank_ref, hits):
    slots = sums_ref.shape[0]
    tasks_here = integrals_ref.shape[0]
    list_length = int(round(slots**0.5))

    @pl.when(pl.program_id(0) == 0)
    def _():
        pair = tasks_ref[0:1, :] * list_length + tasks_ref[1:2, :]
        spot = lax.broadcasted_iota(jnp.int32, (1, tasks_here), 1)
        pair = jnp.where(spot < count_ref[0], pair, -1)
        row = lax.broadcasted_iota(jnp.int32, (slots, tasks_here), 0)
        hits[...] = jnp.where(row == pair, 1.0, 0.0).astype(BF16)

    blank_ref[...] = jnp.zeros_like(blank_ref)
    rows = integrals_ref[...]
    high = rows.astype(BF16)
    low = (rows - high.astype(F32)).astype(BF16)
    sums_ref[...] = jnp.dot(hits[...], high, preferred_element_type=F32) + jnp.dot(
        hits[...], low, preferred_element_type=F32
    )


def product_kernel(owners, amp_from, amp_self, res_to, operator, amplitudes, *rest):
    arrived, outs = rest[: owners - 1], rest[owners - 1 : 2 * owners - 1]
    own, high, low, totals, sems = rest[2 * owners - 1 :]
    rows, columns = high.shape

    def fetch(k):
        source = amplitudes.at[amp_self[k]]
        return pltpu.make_async_copy(source, own.at[k], sems.at[k])

    def split(d, k):
        g = amp_from[d * CAP + k]

        @pl.when(g >= 0)
        def _():
            if d == 0:
                fetch(k).wait()
                values = own[k]
            else:
                values = arrived[d - 1][k]
            top = values.astype(BF16)
            spot = pl.ds(pl.multiple_of(g * TW, TW), TW)
            high[spot, :] = top
            low[spot, :] = (values - top.astype(F32)).astype(BF16)

    for k in range(CAP):
        pl.when(amp_from[k] >= 0)(fetch(k).start)
    for d in range(owners - 1, -1, -1):
        for k in range(CAP):
            split(d, k)
    step = min(rows, 8 * TW)

    @pl.loop(0, rows // step)
    def _(i):
        left = operator[pl.ds(pl.multiple_of(i * step, step), step), :]
        left_high = left.astype(BF16)
        left_low = (left - left_high.astype(F32)).astype(BF16)
        total = jnp.dot(left_high, low[...], preferred_element_type=F32)
        total += jnp.dot(left_low, high[...], preferred_element_type=F32)
        total += jnp.dot(left_high, high[...], preferred_element_type=F32)
        totals[pl.ds(i * (step // TW), step // TW)] = total.reshape(step // TW, TW, columns)

    for d in range(owners):
        for k in range(CAP):
            g = res_to[d * CAP + k]

            @pl.when(g >= 0)
            def _():
                outs[d][k] = totals[g]


def final_kernel(owners, tiles, res_from, res_tile, res_first, window, pair, virt, *rest):
    arrived, (_, out, sums, sems) = rest[:owners], rest[-4:]
    spots = [(d, k, d * CAP + k) for d in range(owners) for k in range(CAP)]
    for d, k, spot in spots:
        first = res_first[spot]

        @pl.when(first == spot)
        def _():
            sums[spot] = arrived[d][k]

        @pl.when((first >= 0) & (first < spot))
        def _():
            sums[first] = sums[first] + arrived[d][k]

    def write(spot):
        return pltpu.make_async_copy(sums.at[spot], out.at[jnp.maximum(res_from[spot], 0)], sems.at[spot])

    for d, k, spot in spots:

        @pl.when(res_first[spot] == spot)
        def _():
            tile = res_tile[spot]
            base = pair[...] - window[tile // tiles]
            below = base - jnp.concatenate([virt[tile % tiles]] * (base.shape[1] // 128), axis=1)
            sums[spot] = sums[spot] / below
            write(spot).start()

    for d, k, spot in spots:
        pl.when(res_first[spot] == spot)(write(spot).wait)


def local(
    tasks,
    task_count,
    integrals,
    amplitudes,
    amp_slot,
    need_amp,
    res_slot,
    needed_residual_tiles,
    pair_energy,
    virt_energy,
    window_energy,
):
    owners = lax.axis_size("tile")
    me = lax.axis_index("tile").astype(jnp.int32)
    per_amp, _, row_count = amplitudes.shape
    per_res = res_slot.shape[0] // owners
    list_length = need_amp.shape[0]
    tile_count = virt_energy.shape[0] // TW
    slots = list_length * list_length
    task_slots = tasks.shape[1]

    own_lists = jnp.concatenate([need_amp, needed_residual_tiles])
    spots = jnp.arange(owners, dtype=jnp.int32)[:, None] == me
    lists = lax.psum(jnp.where(spots, own_lists[None, :], 0), "tile").reshape(-1)
    me_ref = me.reshape(1)

    def exchange(buffers):
        moved = {}
        for d in range(owners - 1, 0, -1):
            moved[d] = lax.ppermute(buffers[d - 1], "tile", [(i, i ^ d) for i in range(owners)])
        return [moved[d] for d in range(1, owners)]

    piece = pltpu.VMEM((CAP, TW, row_count), F32)
    packed = pl.pallas_call(
        functools.partial(pack_kernel, owners, per_amp),
        out_shape=[piece] * (owners - 1),
        in_specs=[SMEM_SPEC] * 3 + [HBM_SPEC],
        out_specs=[VMEM_SPEC] * (owners - 1),
        scratch_shapes=[
            pltpu.SMEM((owners * CAP + 1,), jnp.int32),
            pltpu.SemaphoreType.DMA((owners * CAP,)),
        ],
        compiler_params=params(),
        cost_estimate=cost(0, 2 * list_length * TW * row_count * 4),
        name="pack_tiles",
    )(me_ref, lists, amp_slot, amplitudes)
    fetched = exchange(packed)

    small = jax.ShapeDtypeStruct((owners * CAP,), jnp.int32)
    amp_from, amp_self, res_to, res_from, res_tile, res_first = pl.pallas_call(
        functools.partial(maps_kernel, owners, per_amp, per_res),
        out_shape=[small, jax.ShapeDtypeStruct((CAP,), jnp.int32), small, small, small, small],
        in_specs=[SMEM_SPEC] * 4,
        out_specs=[SMEM_SPEC] * 6,
        scratch_shapes=[pltpu.SMEM((owners,), jnp.int32), pltpu.SMEM((per_res,), jnp.int32)],
        compiler_params=params(),
        name="list_maps",
    )(me_ref, lists, amp_slot, res_slot)

    block = 512
    steps = TW * TW // block
    blank_rows = per_res * TW // steps
    sums, blank = pl.pallas_call(
        sum_kernel,
        grid=(steps,),
        out_shape=[
            jax.ShapeDtypeStruct((slots, TW * TW), F32),
            jax.ShapeDtypeStruct((per_res * TW, row_count), F32),
        ],
        in_specs=[
            SMEM_SPEC,
            pl.BlockSpec((2, task_slots), lambda i: (0, 0)),
            pl.BlockSpec((task_slots, block), lambda i: (0, i)),
        ],
        out_specs=[
            pl.BlockSpec((slots, block), lambda i: (0, i)),
            pl.BlockSpec((blank_rows, row_count), lambda i: (i, 0)),
        ],
        scratch_shapes=[pltpu.VMEM((slots, task_slots), BF16)],
        compiler_params=params(),
        cost_estimate=cost(4 * slots * task_slots * TW * TW, (task_slots + slots) * TW * TW * 4),
        name="sum_integrals",
    )(task_count, tasks, integrals)
    operator = (
        sums.reshape(list_length, list_length, TW, TW)
        .transpose(0, 2, 1, 3)
        .reshape(list_length * TW, list_length * TW)
    )

    virt = jnp.broadcast_to(virt_energy.reshape(tile_count, TW, 1), (tile_count, TW, 128))
    pair = pair_energy.reshape(1, row_count)
    blank = blank.reshape(per_res, TW, row_count)
    operator, virt, pair = lax.optimization_barrier((operator, virt, pair))
    depth = list_length * TW
    products = pl.pallas_call(
        functools.partial(product_kernel, owners),
        out_shape=[piece] * owners,
        in_specs=[SMEM_SPEC] * 3 + [VMEM_SPEC, HBM_SPEC] + [VMEM_SPEC] * (owners - 1),
        out_specs=[VMEM_SPEC] * owners,
        scratch_shapes=[
            pltpu.VMEM((CAP, TW, row_count), F32),
            pltpu.VMEM((depth, row_count), BF16),
            pltpu.VMEM((depth, row_count), BF16),
            pltpu.VMEM((list_length, TW, row_count), F32),
            pltpu.SemaphoreType.DMA((CAP,)),
        ],
        compiler_params=params(),
        cost_estimate=cost(6 * depth * depth * row_count, 4 * depth * (depth + 2 * row_count)),
        name="multiply_tiles",
    )(amp_from, amp_self, res_to, operator, amplitudes, *fetched)
    returned = [products[0]] + exchange(products[1:])
    return pl.pallas_call(
        functools.partial(final_kernel, owners, tile_count),
        out_shape=jax.ShapeDtypeStruct((per_res, TW, row_count), F32),
        in_specs=[SMEM_SPEC] * 4 + [VMEM_SPEC] * (2 + owners) + [HBM_SPEC],
        out_specs=HBM_SPEC,
        scratch_shapes=[
            pltpu.VMEM((owners * CAP, TW, row_count), F32),
            pltpu.SemaphoreType.DMA((owners * CAP,)),
        ],
        input_output_aliases={6 + owners: 0},
        compiler_params=params(),
        cost_estimate=cost(0, per_res * TW * row_count * 4),
        name="finish_tiles",
    )(res_from, res_tile, res_first, window_energy, pair, virt, *returned, blank)


def solution(mesh):
    in_specs = (
        P(None, ("mol", "tile")),
        P(("mol", "tile")),
        P(("mol", "tile"), None),
        P(("mol", "tile"), None, "rep"),
        P("mol"),
        P(("mol", "tile")),
        P("mol"),
        P(("mol", "tile")),
        P(("mol", "rep")),
        P("mol"),
        P("mol"),
    )
    out_specs = P(("mol", "tile"), None, "rep")
    return jax.shard_map(local, mesh=mesh, in_specs=in_specs, out_specs=out_specs, check_vma=False)
```

```python
import functools

import jax
import jax.numpy as jnp
from jax import lax
from jax.experimental import pallas as pl
from jax.experimental.pallas import tpu as pltpu
from jax.sharding import PartitionSpec as P

TW = 64
CAP = 2
VMEM_LIMIT = 56 * 1024 * 1024
F32 = jnp.float32
BF16 = jnp.bfloat16

HBM_SPEC = pl.BlockSpec(memory_space=pl.ANY)
SMEM_SPEC = pl.BlockSpec(memory_space=pltpu.SMEM)
VMEM_SPEC = pl.BlockSpec(memory_space=pltpu.VMEM)


def class_order(owners):
    half = owners // 2
    far = [owners - 2, *range(half, owners - 2), owners - 1]
    near = [*range(2, half), 1]
    return [d for pair in zip(far, near) for d in pair] + far[len(near) :]


def params(limit=VMEM_LIMIT):
    return pltpu.CompilerParams(vmem_limit_bytes=limit)


def cost(flops, touched):
    return pl.CostEstimate(flops=flops, bytes_accessed=touched, transcendentals=0)


def clear(ref, count, value):
    @pl.loop(0, count)
    def _(i):
        ref[i] = value


def pack_kernel(owners, per_owner, me_ref, lists_ref, amp_slot_ref, amplitudes, *rest):
    outs, (picked, sems) = rest[: owners - 1], rest[-2:]
    list_length = lists_ref.shape[0] // owners // 2
    me = me_ref[0]
    low = me * per_owner
    clear(picked, owners * CAP, -1)

    @pl.loop(0, owners)
    def _(partner):
        def note(j, count):
            local = amp_slot_ref[lists_ref[partner * 2 * list_length + j]] - low
            mine = (local >= 0) & (local < per_owner)
            picked[jnp.where(mine, partner * CAP + count, owners * CAP)] = local
            return count + mine.astype(jnp.int32)

        lax.fori_loop(0, list_length, note, jnp.int32(0), unroll=8)

    for step in ("start", "wait"):
        for d in range(owners - 1, 0, -1):
            for k in range(CAP):
                local = picked[jnp.bitwise_xor(me, d) * CAP + k]
                moved = pltpu.make_async_copy(
                    amplitudes.at[jnp.maximum(local, 0)], outs[d - 1].at[k], sems.at[d * CAP + k]
                )
                pl.when(local >= 0)(getattr(moved, step))


def maps_kernel(
    owners, per_amp, per_res, me_ref, lists_ref, amp_slot_ref, res_slot_ref,
    amp_from, amp_self, res_to, res_from, res_tile, res_first, seen, taken,
):
    list_length = lists_ref.shape[0] // owners // 2
    me = me_ref[0]
    for ref in (amp_from, res_to, res_from):
        clear(ref, owners * CAP, -1)
    clear(amp_self, CAP, 0)
    clear(res_tile, owners * CAP, 0)
    clear(res_first, owners * CAP, -1)
    clear(taken, per_res, -1)

    def own_list(offset, slot_map, per_owner, place):
        clear(seen, owners, 0)

        @pl.loop(0, list_length)
        def _(g):
            slot = slot_map[lists_ref[me * 2 * list_length + offset + g]]
            owner = slot // per_owner
            d = jnp.bitwise_xor(owner, me)
            count = seen[d]
            place(d * CAP + count, g, slot - owner * per_owner, d, count)
            seen[d] = count + 1

    def place_amp(at, g, local, d, count):
        amp_from[at] = g

        @pl.when(d == 0)
        def _():
            amp_self[count] = local

    def place_res(at, g, local, d, count):
        res_to[at] = g

    own_list(0, amp_slot_ref, per_amp, place_amp)
    own_list(list_length, res_slot_ref, per_res, place_res)
    clear(seen, owners, 0)
    low = me * per_res

    @pl.loop(0, owners * list_length)
    def _(i):
        partner = i // list_length
        tile = lists_ref[partner * 2 * list_length + list_length + i % list_length]
        local = res_slot_ref[tile] - low

        @pl.when((local >= 0) & (local < per_res))
        def _():
            d = jnp.bitwise_xor(partner, me)
            count = seen[d]
            res_from[d * CAP + count] = local
            res_tile[d * CAP + count] = tile
            seen[d] = count + 1

    @pl.loop(0, owners * CAP)
    def _(spot):
        local = res_from[spot]

        @pl.when(local >= 0)
        def _():
            @pl.when(taken[local] < 0)
            def _():
                taken[local] = spot

            res_first[spot] = taken[local]


def sum_kernel(count_ref, tasks_ref, integrals_ref, sums_ref, blank_ref, hits):
    slots = sums_ref.shape[0]
    tasks_here = integrals_ref.shape[0]
    list_length = int(round(slots**0.5))

    @pl.when(pl.program_id(0) == 0)
    def _():
        pair = tasks_ref[0:1, :] * list_length + tasks_ref[1:2, :]
        spot = lax.broadcasted_iota(jnp.int32, (1, tasks_here), 1)
        pair = jnp.where(spot < count_ref[0], pair, -1)
        row = lax.broadcasted_iota(jnp.int32, (slots, tasks_here), 0)
        hits[...] = jnp.where(row == pair, 1.0, 0.0).astype(BF16)

    blank_ref[...] = jnp.zeros_like(blank_ref)
    rows = integrals_ref[...]
    high = rows.astype(BF16)
    low = (rows - high.astype(F32)).astype(BF16)
    sums_ref[...] = jnp.dot(hits[...], high, preferred_element_type=F32) + jnp.dot(
        hits[...], low, preferred_element_type=F32
    )


def product_kernel(owners, amp_from, amp_self, res_to, operator, amplitudes, *rest):
    arrived, outs = dict(zip(class_order(owners), rest[: owners - 1])), rest[owners - 1 : 2 * owners - 1]
    own, high, low, totals, sems = rest[2 * owners - 1 :]
    rows, columns = high.shape

    def fetch(k):
        source = amplitudes.at[amp_self[k]]
        return pltpu.make_async_copy(source, own.at[k], sems.at[k])

    def split(d, k):
        g = amp_from[d * CAP + k]

        @pl.when(g >= 0)
        def _():
            if d == 0:
                fetch(k).wait()
                values = own[k]
            else:
                values = arrived[d][k]
            top = values.astype(BF16)
            spot = pl.ds(pl.multiple_of(g * TW, TW), TW)
            high[spot, :] = top
            low[spot, :] = (values - top.astype(F32)).astype(BF16)

    for k in range(CAP):
        pl.when(amp_from[k] >= 0)(fetch(k).start)
    for d in range(owners - 1, -1, -1):
        for k in range(CAP):
            split(d, k)
    step = min(rows, 8 * TW)

    @pl.loop(0, rows // step)
    def _(i):
        left = operator[pl.ds(pl.multiple_of(i * step, step), step), :]
        left_high = left.astype(BF16)
        left_low = (left - left_high.astype(F32)).astype(BF16)
        total = jnp.dot(left_high, low[...], preferred_element_type=F32)
        total += jnp.dot(left_low, high[...], preferred_element_type=F32)
        total += jnp.dot(left_high, high[...], preferred_element_type=F32)
        totals[pl.ds(i * (step // TW), step // TW)] = total.reshape(step // TW, TW, columns)

    for d in range(owners):
        for k in range(CAP):
            g = res_to[d * CAP + k]

            @pl.when(g >= 0)
            def _():
                outs[d][k] = totals[g]


def final_kernel(owners, tiles, res_from, res_tile, res_first, window, pair, virt, *rest):
    arrived, (_, out, sums, sems) = dict(zip([0] + class_order(owners), rest[:owners])), rest[-4:]
    spots = [(d, k, d * CAP + k) for d in range(owners) for k in range(CAP)]
    for d, k, spot in spots:
        first = res_first[spot]

        @pl.when(first == spot)
        def _():
            sums[spot] = arrived[d][k]

        @pl.when((first >= 0) & (first < spot))
        def _():
            sums[first] = sums[first] + arrived[d][k]

    def write(spot):
        return pltpu.make_async_copy(sums.at[spot], out.at[jnp.maximum(res_from[spot], 0)], sems.at[spot])

    for d, k, spot in spots:

        @pl.when(res_first[spot] == spot)
        def _():
            tile = res_tile[spot]
            base = pair[...] - window[tile // tiles]
            below = base - jnp.concatenate([virt[tile % tiles]] * (base.shape[1] // 128), axis=1)
            sums[spot] = sums[spot] / below
            write(spot).start()

    for d, k, spot in spots:
        pl.when(res_first[spot] == spot)(write(spot).wait)


def local(
    tasks,
    task_count,
    integrals,
    amplitudes,
    amp_slot,
    need_amp,
    res_slot,
    needed_residual_tiles,
    pair_energy,
    virt_energy,
    window_energy,
):
    owners = lax.axis_size("tile")
    me = lax.axis_index("tile").astype(jnp.int32)
    per_amp, _, row_count = amplitudes.shape
    per_res = res_slot.shape[0] // owners
    list_length = need_amp.shape[0]
    tile_count = virt_energy.shape[0] // TW
    slots = list_length * list_length
    task_slots = tasks.shape[1]

    own_lists = jnp.concatenate([need_amp, needed_residual_tiles])
    spots = jnp.arange(owners, dtype=jnp.int32)[:, None] == me
    lists = lax.psum(jnp.where(spots, own_lists[None, :], 0), "tile").reshape(-1)
    me_ref = me.reshape(1)

    def exchange(buffers):
        return [lax.ppermute(buffers[d - 1], "tile", [(i, i ^ d) for i in range(owners)]) for d in class_order(owners)]

    piece = pltpu.VMEM((CAP, TW, row_count), F32)
    packed = pl.pallas_call(
        functools.partial(pack_kernel, owners, per_amp),
        out_shape=[piece] * (owners - 1),
        in_specs=[SMEM_SPEC] * 3 + [HBM_SPEC],
        out_specs=[VMEM_SPEC] * (owners - 1),
        scratch_shapes=[
            pltpu.SMEM((owners * CAP + 1,), jnp.int32),
            pltpu.SemaphoreType.DMA((owners * CAP,)),
        ],
        compiler_params=params(),
        cost_estimate=cost(0, 2 * list_length * TW * row_count * 4),
        name="pack_tiles",
    )(me_ref, lists, amp_slot, amplitudes)
    fetched = exchange(packed)

    small = jax.ShapeDtypeStruct((owners * CAP,), jnp.int32)
    amp_from, amp_self, res_to, res_from, res_tile, res_first = pl.pallas_call(
        functools.partial(maps_kernel, owners, per_amp, per_res),
        out_shape=[small, jax.ShapeDtypeStruct((CAP,), jnp.int32), small, small, small, small],
        in_specs=[SMEM_SPEC] * 4,
        out_specs=[SMEM_SPEC] * 6,
        scratch_shapes=[pltpu.SMEM((owners,), jnp.int32), pltpu.SMEM((per_res,), jnp.int32)],
        compiler_params=params(),
        name="list_maps",
    )(me_ref, lists, amp_slot, res_slot)

    block = 512
    steps = TW * TW // block
    blank_rows = per_res * TW // steps
    sums, blank = pl.pallas_call(
        sum_kernel,
        grid=(steps,),
        out_shape=[
            jax.ShapeDtypeStruct((slots, TW * TW), F32),
            jax.ShapeDtypeStruct((per_res * TW, row_count), F32),
        ],
        in_specs=[
            SMEM_SPEC,
            pl.BlockSpec((2, task_slots), lambda i: (0, 0)),
            pl.BlockSpec((task_slots, block), lambda i: (0, i)),
        ],
        out_specs=[
            pl.BlockSpec((slots, block), lambda i: (0, i)),
            pl.BlockSpec((blank_rows, row_count), lambda i: (i, 0)),
        ],
        scratch_shapes=[pltpu.VMEM((slots, task_slots), BF16)],
        compiler_params=params(),
        cost_estimate=cost(4 * slots * task_slots * TW * TW, (task_slots + slots) * TW * TW * 4),
        name="sum_integrals",
    )(task_count, tasks, integrals)
    operator = (
        sums.reshape(list_length, list_length, TW, TW)
        .transpose(0, 2, 1, 3)
        .reshape(list_length * TW, list_length * TW)
    )

    virt = jnp.broadcast_to(virt_energy.reshape(tile_count, TW, 1), (tile_count, TW, 128))
    pair = pair_energy.reshape(1, row_count)
    blank = blank.reshape(per_res, TW, row_count)
    operator, virt, pair = lax.optimization_barrier((operator, virt, pair))
    depth = list_length * TW
    products = pl.pallas_call(
        functools.partial(product_kernel, owners),
        out_shape=[piece] * owners,
        in_specs=[SMEM_SPEC] * 3 + [VMEM_SPEC, HBM_SPEC] + [VMEM_SPEC] * (owners - 1),
        out_specs=[VMEM_SPEC] * owners,
        scratch_shapes=[
            pltpu.VMEM((CAP, TW, row_count), F32),
            pltpu.VMEM((depth, row_count), BF16),
            pltpu.VMEM((depth, row_count), BF16),
            pltpu.VMEM((list_length, TW, row_count), F32),
            pltpu.SemaphoreType.DMA((CAP,)),
        ],
        compiler_params=params(),
        cost_estimate=cost(6 * depth * depth * row_count, 4 * depth * (depth + 2 * row_count)),
        name="multiply_tiles",
    )(amp_from, amp_self, res_to, operator, amplitudes, *fetched)
    returned = [products[0]] + exchange(products[1:])
    return pl.pallas_call(
        functools.partial(final_kernel, owners, tile_count),
        out_shape=jax.ShapeDtypeStruct((per_res, TW, row_count), F32),
        in_specs=[SMEM_SPEC] * 4 + [VMEM_SPEC] * (2 + owners) + [HBM_SPEC],
        out_specs=HBM_SPEC,
        scratch_shapes=[
            pltpu.VMEM((owners * CAP, TW, row_count), F32),
            pltpu.SemaphoreType.DMA((owners * CAP,)),
        ],
        input_output_aliases={6 + owners: 0},
        compiler_params=params(),
        cost_estimate=cost(0, per_res * TW * row_count * 4),
        name="finish_tiles",
    )(res_from, res_tile, res_first, window_energy, pair, virt, *returned, blank)


def solution(mesh):
    in_specs = (
        P(None, ("mol", "tile")),
        P(("mol", "tile")),
        P(("mol", "tile"), None),
        P(("mol", "tile"), None, "rep"),
        P("mol"),
        P(("mol", "tile")),
        P("mol"),
        P(("mol", "tile")),
        P(("mol", "rep")),
        P("mol"),
        P("mol"),
    )
    out_specs = P(("mol", "tile"), None, "rep")
    return jax.shard_map(local, mesh=mesh, in_specs=in_specs, out_specs=out_specs, check_vma=False)
```

```python
import functools

import jax
import jax.numpy as jnp
from jax import lax
from jax.experimental import pallas as pl
from jax.experimental.pallas import tpu as pltpu
from jax.sharding import PartitionSpec as P

TW = 64
CAP = 2
VMEM_LIMIT = 32 * 1024 * 1024
F32 = jnp.float32
BF16 = jnp.bfloat16

HBM_SPEC = pl.BlockSpec(memory_space=pl.ANY)
SMEM_SPEC = pl.BlockSpec(memory_space=pltpu.SMEM)
VMEM_SPEC = pl.BlockSpec(memory_space=pltpu.VMEM)


def class_order(owners):
    half = owners // 2
    far = [owners - 2, *range(half, owners - 2), owners - 1]
    near = [*range(2, half), 1]
    return [d for pair in zip(far, near) for d in pair] + far[len(near) :]


def params(limit=VMEM_LIMIT):
    return pltpu.CompilerParams(vmem_limit_bytes=limit)


def cost(flops, touched):
    return pl.CostEstimate(flops=flops, bytes_accessed=touched, transcendentals=0)


def in_vmem(array):
    return pltpu.with_memory_space_constraint(array, pltpu.VMEM)


def clear(ref, count, value):
    @pl.loop(0, count)
    def _(i):
        ref[i] = value


def pack_kernel(owners, per_owner, me_ref, lists_ref, amp_slot_ref, amplitudes, *rest):
    outs, (picked, sems) = rest[: owners - 1], rest[-2:]
    list_length = lists_ref.shape[0] // owners // 2
    me = me_ref[0]
    low = me * per_owner
    clear(picked, owners * CAP, -1)

    @pl.loop(0, owners)
    def _(partner):
        def note(j, count):
            local = amp_slot_ref[lists_ref[partner * 2 * list_length + j]] - low
            mine = (local >= 0) & (local < per_owner)
            picked[jnp.where(mine, partner * CAP + count, owners * CAP)] = local
            return count + mine.astype(jnp.int32)

        lax.fori_loop(0, list_length, note, jnp.int32(0), unroll=8)

    for step in ("start", "wait"):
        for d in range(owners - 1, 0, -1):
            for k in range(CAP):
                local = picked[jnp.bitwise_xor(me, d) * CAP + k]
                moved = pltpu.make_async_copy(
                    amplitudes.at[jnp.maximum(local, 0)], outs[d - 1].at[k], sems.at[d * CAP + k]
                )
                pl.when(local >= 0)(getattr(moved, step))


def maps_kernel(
    owners, per_amp, per_res, me_ref, lists_ref, amp_slot_ref, res_slot_ref,
    amp_from, amp_self, res_to, res_from, res_tile, res_first, seen, taken,
):
    list_length = lists_ref.shape[0] // owners // 2
    spots = owners * CAP
    me = me_ref[0]
    for ref in (amp_from, res_to, res_from):
        clear(ref, spots, -1)
    clear(amp_self, CAP + 1, 0)
    clear(res_tile, spots, 0)
    clear(taken, per_res + 1, -1)

    def own_list(offset, slot_map, per_owner, place, self_slots):
        clear(seen, owners, 0)

        def note(g, carry):
            slot = slot_map[lists_ref[me * 2 * list_length + offset + g]]
            owner = lax.div(slot, jnp.int32(per_owner))
            d = jnp.bitwise_xor(owner, me)
            count = seen[d]
            place[d * CAP + count] = g
            seen[d] = count + 1
            if self_slots is not None:
                self_slots[jnp.where(d == 0, count, CAP)] = slot - owner * per_owner
            return carry

        lax.fori_loop(0, list_length, note, 0, unroll=8)

    own_list(0, amp_slot_ref, per_amp, amp_from, amp_self)
    own_list(list_length, res_slot_ref, per_res, res_to, None)
    low = me * per_res

    @pl.loop(0, owners)
    def _(partner):
        d = jnp.bitwise_xor(partner, me)

        def note(j, count):
            tile = lists_ref[partner * 2 * list_length + list_length + j]
            local = res_slot_ref[tile] - low
            mine = (local >= 0) & (local < per_res)
            spot = jnp.where(mine, d * CAP + count, spots)
            res_from[spot] = local
            res_tile[spot] = tile
            return count + mine.astype(jnp.int32)

        lax.fori_loop(0, list_length, note, jnp.int32(0), unroll=8)

    def firsts(spot, carry):
        local = res_from[spot]
        known = taken[jnp.where(local >= 0, local, per_res)]
        first = jnp.where(known < 0, spot, known)
        taken[jnp.where(local >= 0, local, per_res)] = jnp.where(local >= 0, first, -1)
        res_first[spot] = jnp.where(local >= 0, first, -1)
        return carry

    lax.fori_loop(0, spots, firsts, 0, unroll=4)


def sum_kernel(list_length, count_ref, tasks_ref, integrals_ref, high_ref, low_ref, blank_ref, hits, sums, matrix):
    slots = list_length * list_length
    tasks_here, block = integrals_ref.shape

    @pl.when(pl.program_id(0) == 0)
    def _():
        pair = tasks_ref[0:1, :] * list_length + tasks_ref[1:2, :]
        spot = lax.broadcasted_iota(jnp.int32, (1, tasks_here), 1)
        pair = jnp.where(spot < count_ref[0], pair, -1)
        row = lax.broadcasted_iota(jnp.int32, (slots, tasks_here), 0)
        hits[...] = jnp.where(row == pair, 1.0, 0.0).astype(BF16)

    blank_ref[...] = jnp.zeros_like(blank_ref)
    rows = integrals_ref[...]
    high = rows.astype(BF16)
    low = (rows - high.astype(F32)).astype(BF16)
    found = jnp.dot(hits[...], high, preferred_element_type=F32) + jnp.dot(
        hits[...], low, preferred_element_type=F32
    )
    for i in range(0, block // TW, 2):
        sums[i // 2] = found[:, i * TW : (i + 2) * TW]
    left = lax.broadcasted_iota(jnp.int32, (list_length, 2 * TW), 1) < TW
    for i in range(0, block // TW, 2):
        for a in range(0, list_length, 2):
            even = sums[i // 2, pl.ds(a, list_length, stride=list_length), :]
            odd = sums[i // 2, pl.ds(a + 1, list_length, stride=list_length), :]
            lanes = pl.ds(a * TW, 2 * TW)
            matrix[pl.ds(i * list_length, list_length), lanes] = jnp.where(left, even, pltpu.roll(odd, TW, 1))
            matrix[pl.ds((i + 1) * list_length, list_length), lanes] = jnp.where(left, pltpu.roll(even, TW, 1), odd)
    whole = matrix[...]
    top = whole.astype(BF16)
    high_ref[...] = top
    low_ref[...] = (whole - top.astype(F32)).astype(BF16)


def product_kernel(owners, amp_from, amp_self, res_to, operator_high, operator_low, amplitudes, *rest):
    arrived, outs = dict(zip(class_order(owners), rest[: owners - 1])), rest[owners - 1 : 2 * owners - 1]
    own, high, low, totals, sems = rest[2 * owners - 1 :]
    rows, columns = high.shape

    def fetch(k):
        source = amplitudes.at[amp_self[k]]
        return pltpu.make_async_copy(source, own.at[k], sems.at[k])

    def split(d, k):
        g = amp_from[d * CAP + k]

        @pl.when(g >= 0)
        def _():
            if d == 0:
                fetch(k).wait()
                values = own[k]
            else:
                values = arrived[d][k]
            top = values.astype(BF16)
            spot = pl.ds(pl.multiple_of(g * TW, TW), TW)
            high[spot, :] = top
            low[spot, :] = (values - top.astype(F32)).astype(BF16)

    for k in range(CAP):
        pl.when(amp_from[k] >= 0)(fetch(k).start)
    for d in range(owners - 1, -1, -1):
        for k in range(CAP):
            split(d, k)
    step = min(rows, 8 * TW)

    @pl.loop(0, rows // step)
    def _(i):
        here = pl.ds(pl.multiple_of(i * step, step), step)
        total = jnp.dot(operator_high[here, :], low[...], preferred_element_type=F32)
        total += jnp.dot(operator_low[here, :], high[...], preferred_element_type=F32)
        total += jnp.dot(operator_high[here, :], high[...], preferred_element_type=F32)
        for c in range(columns // 128):
            totals[c, here, :] = total[:, c * 128 : (c + 1) * 128]

    for d in range(owners):
        for k in range(CAP):
            g = res_to[d * CAP + k]

            @pl.when(g >= 0)
            def _():
                for c in range(columns // 128):
                    outs[d][k, :, c * 128 : (c + 1) * 128] = totals[c, pl.ds(g, TW, stride=rows // TW), :]


def final_kernel(owners, tiles, res_from, res_tile, res_first, window, pair, virt, *rest):
    arrived, (_, out, sums, sems) = dict(zip([0] + class_order(owners), rest[:owners])), rest[-4:]
    spots = [(d, k, d * CAP + k) for d in range(owners) for k in range(CAP)]
    for d, k, spot in spots:
        first = res_first[spot]

        @pl.when(first == spot)
        def _():
            sums[spot] = arrived[d][k]

        @pl.when((first >= 0) & (first < spot))
        def _():
            sums[first] = sums[first] + arrived[d][k]

    def write(spot):
        return pltpu.make_async_copy(sums.at[spot], out.at[jnp.maximum(res_from[spot], 0)], sems.at[spot])

    for d, k, spot in spots:

        @pl.when(res_first[spot] == spot)
        def _():
            tile = res_tile[spot]
            base = pair[...] - window[tile // tiles]
            below = base - jnp.concatenate([virt[tile % tiles]] * (base.shape[1] // 128), axis=1)
            sums[spot] = sums[spot] / below
            write(spot).start()

    for d, k, spot in spots:
        pl.when(res_first[spot] == spot)(write(spot).wait)


def local(
    tasks,
    task_count,
    integrals,
    amplitudes,
    amp_slot,
    need_amp,
    res_slot,
    needed_residual_tiles,
    pair_energy,
    virt_energy,
    window_energy,
):
    owners = lax.axis_size("tile")
    me = lax.axis_index("tile").astype(jnp.int32)
    per_amp, _, row_count = amplitudes.shape
    per_res = res_slot.shape[0] // owners
    list_length = need_amp.shape[0]
    tile_count = virt_energy.shape[0] // TW
    slots = list_length * list_length
    task_slots = tasks.shape[1]

    amplitudes = pltpu.with_memory_space_constraint(amplitudes, pltpu.HBM)
    integrals = pltpu.with_memory_space_constraint(integrals, pltpu.HBM)
    own_lists = jnp.concatenate([need_amp, needed_residual_tiles])
    spots = jnp.arange(owners, dtype=jnp.int32)[:, None] == me
    lists = lax.psum(jnp.where(spots, own_lists[None, :], 0), "tile").reshape(-1)
    me_ref = me.reshape(1)

    def exchange(buffers):
        return [
            in_vmem(lax.ppermute(buffers[d - 1], "tile", [(i, i ^ d) for i in range(owners)]))
            for d in class_order(owners)
        ]

    piece = pltpu.VMEM((CAP, TW, row_count), F32)
    packed = pl.pallas_call(
        functools.partial(pack_kernel, owners, per_amp),
        out_shape=[piece] * (owners - 1),
        in_specs=[SMEM_SPEC] * 3 + [HBM_SPEC],
        out_specs=[VMEM_SPEC] * (owners - 1),
        scratch_shapes=[
            pltpu.SMEM((owners * CAP + 1,), jnp.int32),
            pltpu.SemaphoreType.DMA((owners * CAP,)),
        ],
        compiler_params=params(),
        cost_estimate=cost(0, 2 * list_length * TW * row_count * 4),
        name="pack_tiles",
    )(me_ref, lists, amp_slot, amplitudes)
    fetched = exchange(packed)

    small = pltpu.SMEM((owners * CAP + 1,), jnp.int32)
    amp_from, amp_self, res_to, res_from, res_tile, res_first = pl.pallas_call(
        functools.partial(maps_kernel, owners, per_amp, per_res),
        out_shape=[small, pltpu.SMEM((CAP + 1,), jnp.int32), small, small, small, small],
        in_specs=[SMEM_SPEC] * 4,
        out_specs=[SMEM_SPEC] * 6,
        scratch_shapes=[pltpu.SMEM((owners,), jnp.int32), pltpu.SMEM((per_res + 1,), jnp.int32)],
        compiler_params=params(),
        name="list_maps",
    )(me_ref, lists, amp_slot, res_slot)

    amp_from, amp_self, res_to, res_from, res_tile, res_first = (
        pltpu.with_memory_space_constraint(x, pltpu.SMEM)
        for x in (amp_from, amp_self, res_to, res_from, res_tile, res_first)
    )
    block = 1024
    steps = TW * TW // block
    depth = list_length * TW
    operator_rows = depth // steps
    blank_rows = per_res * TW // steps
    keep = depth <= 1024
    operator = pltpu.VMEM((depth, depth), BF16) if keep else jax.ShapeDtypeStruct((depth, depth), BF16)
    operator_high, operator_low, blank = pl.pallas_call(
        functools.partial(sum_kernel, list_length),
        grid=(steps,),
        out_shape=[operator, operator, jax.ShapeDtypeStruct((per_res * TW, row_count), F32)],
        in_specs=[
            SMEM_SPEC,
            pl.BlockSpec((2, task_slots), lambda i: (0, 0)),
            pl.BlockSpec((task_slots, block), lambda i: (0, i)),
        ],
        out_specs=[
            pl.BlockSpec((operator_rows, depth), lambda i: (i, 0)),
            pl.BlockSpec((operator_rows, depth), lambda i: (i, 0)),
            pl.BlockSpec((blank_rows, row_count), lambda i: (i, 0)),
        ],
        scratch_shapes=[
            pltpu.VMEM((slots, task_slots), BF16),
            pltpu.VMEM((block // (2 * TW), slots, 2 * TW), F32),
            pltpu.VMEM((operator_rows, depth), F32),
        ],
        compiler_params=params(),
        cost_estimate=cost(4 * slots * task_slots * TW * TW, (task_slots + slots) * TW * TW * 4),
        name="sum_integrals",
    )(task_count, tasks, integrals)

    virt = jnp.broadcast_to(virt_energy.reshape(tile_count, TW, 1), (tile_count, TW, 128))
    pair = pair_energy.reshape(1, row_count)
    blank = blank.reshape(per_res, TW, row_count)
    operator_high, virt, pair = lax.optimization_barrier((operator_high, virt, pair))
    virt, pair = in_vmem(virt), in_vmem(pair)
    if keep:
        operator_high, operator_low = in_vmem(operator_high), in_vmem(operator_low)
    products = pl.pallas_call(
        functools.partial(product_kernel, owners),
        out_shape=[piece] * owners,
        in_specs=[SMEM_SPEC] * 3 + [VMEM_SPEC] * 2 + [HBM_SPEC] + [VMEM_SPEC] * (owners - 1),
        out_specs=[VMEM_SPEC] * owners,
        scratch_shapes=[
            pltpu.VMEM((CAP, TW, row_count), F32),
            pltpu.VMEM((depth, row_count), BF16),
            pltpu.VMEM((depth, row_count), BF16),
            pltpu.VMEM((row_count // 128, depth, 128), F32),
            pltpu.SemaphoreType.DMA((CAP,)),
        ],
        compiler_params=params(),
        cost_estimate=cost(6 * depth * depth * row_count, 4 * depth * (depth + 2 * row_count)),
        name="multiply_tiles",
    )(amp_from, amp_self, res_to, operator_high, operator_low, amplitudes, *fetched)
    returned = [in_vmem(products[0])] + exchange(products[1:])
    return pl.pallas_call(
        functools.partial(final_kernel, owners, tile_count),
        out_shape=jax.ShapeDtypeStruct((per_res, TW, row_count), F32),
        in_specs=[SMEM_SPEC] * 4 + [VMEM_SPEC] * (2 + owners) + [HBM_SPEC],
        out_specs=HBM_SPEC,
        scratch_shapes=[
            pltpu.VMEM((owners * CAP, TW, row_count), F32),
            pltpu.SemaphoreType.DMA((owners * CAP,)),
        ],
        input_output_aliases={6 + owners: 0},
        compiler_params=params(),
        cost_estimate=cost(0, per_res * TW * row_count * 4),
        name="finish_tiles",
    )(res_from, res_tile, res_first, window_energy, pair, virt, *returned, blank)


def solution(mesh):
    in_specs = (
        P(None, ("mol", "tile")),
        P(("mol", "tile")),
        P(("mol", "tile"), None),
        P(("mol", "tile"), None, "rep"),
        P("mol"),
        P(("mol", "tile")),
        P("mol"),
        P(("mol", "tile")),
        P(("mol", "rep")),
        P("mol"),
        P("mol"),
    )
    out_specs = P(("mol", "tile"), None, "rep")
    return jax.shard_map(local, mesh=mesh, in_specs=in_specs, out_specs=out_specs, check_vma=False)
```

```python
import functools

import jax
import jax.numpy as jnp
from jax import lax
from jax.experimental import pallas as pl
from jax.experimental.pallas import tpu as pltpu
from jax.sharding import PartitionSpec as P

TW = 64
CAP = 2
VMEM_LIMIT = 32 * 1024 * 1024
F32 = jnp.float32
BF16 = jnp.bfloat16

HBM_SPEC = pl.BlockSpec(memory_space=pl.ANY)
SMEM_SPEC = pl.BlockSpec(memory_space=pltpu.SMEM)
VMEM_SPEC = pl.BlockSpec(memory_space=pltpu.VMEM)


def class_order(owners):
    half = owners // 2
    far = [owners - 2, *range(half, owners - 2), owners - 1]
    near = [*range(2, half), 1]
    return [d for pair in zip(far, near) for d in pair] + far[len(near) :]


def params(limit=VMEM_LIMIT):
    return pltpu.CompilerParams(vmem_limit_bytes=limit)


def cost(flops, touched):
    return pl.CostEstimate(flops=flops, bytes_accessed=touched, transcendentals=0)


def in_vmem(array):
    return pltpu.with_memory_space_constraint(array, pltpu.VMEM)


def clear(ref, count, value):
    @pl.loop(0, count)
    def _(i):
        ref[i] = value


def pack_kernel(owners, per_owner, me_ref, lists_ref, amp_slot_ref, amplitudes, *rest):
    outs, (picked, sems) = rest[: owners - 1], rest[-2:]
    list_length = lists_ref.shape[0] // owners // 2
    me = me_ref[0]
    low = me * per_owner
    clear(picked, owners * CAP, -1)

    def copy(d, k):
        local = picked[d * CAP + k]
        source = amplitudes.at[jnp.maximum(local, 0)]
        return local, pltpu.make_async_copy(source, outs[d - 1].at[k], sems.at[d * CAP + k])

    for d in class_order(owners):
        first = jnp.bitwise_xor(me, d) * 2 * list_length

        def note(j, count):
            local = amp_slot_ref[lists_ref[first + j]] - low
            mine = (local >= 0) & (local < per_owner)
            picked[jnp.where(mine, d * CAP + count, owners * CAP)] = local
            return count + mine.astype(jnp.int32)

        lax.fori_loop(0, list_length, note, jnp.int32(0), unroll=8)
        for k in range(CAP):
            local, moved = copy(d, k)
            pl.when(local >= 0)(moved.start)
    for d in class_order(owners):
        for k in range(CAP):
            local, moved = copy(d, k)
            pl.when(local >= 0)(moved.wait)


def maps_kernel(
    owners, per_amp, per_res, me_ref, lists_ref, amp_slot_ref, res_slot_ref,
    window, pair, virt, amp_from, amp_self, res_to, res_from, res_first, inverse, res_tile, seen, taken,
):
    list_length = lists_ref.shape[0] // owners // 2
    spots = owners * CAP
    me = me_ref[0]
    for ref in (amp_from, res_to, res_from):
        clear(ref, spots, -1)
    clear(amp_self, CAP + 1, 0)
    clear(res_tile, spots, 0)
    clear(taken, per_res + 1, -1)

    def own_list(offset, slot_map, per_owner, place, self_slots):
        clear(seen, owners, 0)

        def note(g, carry):
            slot = slot_map[lists_ref[me * 2 * list_length + offset + g]]
            owner = lax.div(slot, jnp.int32(per_owner))
            d = jnp.bitwise_xor(owner, me)
            count = seen[d]
            place[d * CAP + count] = g
            seen[d] = count + 1
            if self_slots is not None:
                self_slots[jnp.where(d == 0, count, CAP)] = slot - owner * per_owner
            return carry

        lax.fori_loop(0, list_length, note, 0, unroll=8)

    own_list(0, amp_slot_ref, per_amp, amp_from, amp_self)
    own_list(list_length, res_slot_ref, per_res, res_to, None)
    low = me * per_res

    @pl.loop(0, owners)
    def _(partner):
        d = jnp.bitwise_xor(partner, me)

        def note(j, count):
            tile = lists_ref[partner * 2 * list_length + list_length + j]
            local = res_slot_ref[tile] - low
            mine = (local >= 0) & (local < per_res)
            spot = jnp.where(mine, d * CAP + count, spots)
            res_from[spot] = local
            res_tile[spot] = tile
            return count + mine.astype(jnp.int32)

        lax.fori_loop(0, list_length, note, jnp.int32(0), unroll=8)

    for d in [0] + class_order(owners):
        for spot in range(d * CAP, d * CAP + CAP):
            local = res_from[spot]
            at = jnp.where(local >= 0, local, per_res)
            first = jnp.where(local < 0, -1, jnp.where(taken[at] < 0, spot, taken[at]))
            taken[at] = first
            res_first[spot] = first

    tiles, columns = virt.shape[0], pair.shape[1]

    @pl.loop(0, spots)
    def _(spot):
        @pl.when(res_from[spot] >= 0)
        def _():
            tile = res_tile[spot]
            base = pair[...] - window[lax.div(tile, jnp.int32(tiles))]
            column = virt[lax.rem(tile, jnp.int32(tiles))]
            inverse[spot] = 1.0 / (base - jnp.concatenate([column] * (columns // 128), axis=1))


def sum_kernel(list_length, count_ref, tasks_ref, integrals_ref, high_ref, low_ref, blank_ref, hits, sums, matrix):
    slots = list_length * list_length
    tasks_here, block = integrals_ref.shape

    @pl.when(pl.program_id(0) == 0)
    def _():
        pair = tasks_ref[0:1, :] * list_length + tasks_ref[1:2, :]
        spot = lax.broadcasted_iota(jnp.int32, (1, tasks_here), 1)
        pair = jnp.where(spot < count_ref[0], pair, -1)
        row = lax.broadcasted_iota(jnp.int32, (slots, tasks_here), 0)
        hits[...] = jnp.where(row == pair, 1.0, 0.0).astype(BF16)

    blank_ref[...] = jnp.zeros_like(blank_ref)
    rows = integrals_ref[...]
    high = rows.astype(BF16)
    low = (rows - high.astype(F32)).astype(BF16)
    found = jnp.dot(hits[...], high, preferred_element_type=F32) + jnp.dot(
        hits[...], low, preferred_element_type=F32
    )
    for i in range(0, block // TW, 2):
        sums[i // 2] = found[:, i * TW : (i + 2) * TW]
    left = lax.broadcasted_iota(jnp.int32, (list_length, 2 * TW), 1) < TW
    for i in range(0, block // TW, 2):
        for a in range(0, list_length, 2):
            even = sums[i // 2, pl.ds(a, list_length, stride=list_length), :]
            odd = sums[i // 2, pl.ds(a + 1, list_length, stride=list_length), :]
            lanes = pl.ds(a * TW, 2 * TW)
            matrix[pl.ds(i * list_length, list_length), lanes] = jnp.where(left, even, pltpu.roll(odd, TW, 1))
            matrix[pl.ds((i + 1) * list_length, list_length), lanes] = jnp.where(left, pltpu.roll(even, TW, 1), odd)
    whole = matrix[...]
    top = whole.astype(BF16)
    high_ref[...] = top
    low_ref[...] = (whole - top.astype(F32)).astype(BF16)


def product_kernel(owners, amp_from, amp_self, res_to, operator_high, operator_low, amplitudes, *rest):
    arrived, outs = dict(zip(class_order(owners), rest[: owners - 1])), rest[owners - 1 : 2 * owners - 1]
    own, high, low, totals, sems = rest[2 * owners - 1 :]
    rows, columns = high.shape

    def fetch(k):
        source = amplitudes.at[amp_self[k]]
        return pltpu.make_async_copy(source, own.at[k], sems.at[k])

    def split(d, k):
        g = amp_from[d * CAP + k]

        @pl.when(g >= 0)
        def _():
            if d == 0:
                fetch(k).wait()
                values = own[k]
            else:
                values = arrived[d][k]
            top = values.astype(BF16)
            spot = pl.ds(pl.multiple_of(g * TW, TW), TW)
            high[spot, :] = top
            low[spot, :] = (values - top.astype(F32)).astype(BF16)

    for k in range(CAP):
        pl.when(amp_from[k] >= 0)(fetch(k).start)
    for d in range(owners - 1, -1, -1):
        for k in range(CAP):
            split(d, k)
    step = min(rows, 8 * TW)

    @pl.loop(0, rows // step)
    def _(i):
        here = pl.ds(pl.multiple_of(i * step, step), step)
        total = jnp.dot(operator_high[here, :], low[...], preferred_element_type=F32)
        total += jnp.dot(operator_low[here, :], high[...], preferred_element_type=F32)
        total += jnp.dot(operator_high[here, :], high[...], preferred_element_type=F32)
        for c in range(columns // 128):
            totals[c, here, :] = total[:, c * 128 : (c + 1) * 128]

    for d in range(owners):
        for k in range(CAP):
            g = res_to[d * CAP + k]

            @pl.when(g >= 0)
            def _():
                for c in range(columns // 128):
                    outs[d][k, :, c * 128 : (c + 1) * 128] = totals[c, pl.ds(g, TW, stride=rows // TW), :]


def final_kernel(owners, res_from, res_first, inverse, *rest):
    arrived, (_, out, sums, sems) = rest[:owners], rest[-4:]
    spots = [(at, k, d * CAP + k) for at, d in enumerate([0] + class_order(owners)) for k in range(CAP)]
    for at, k, spot in spots:
        first = res_first[spot]

        @pl.when(first == spot)
        def _():
            sums[spot] = arrived[at][k] * inverse[spot]

        @pl.when((first >= 0) & (first != spot))
        def _():
            sums[first] = sums[first] + arrived[at][k] * inverse[spot]

    def write(spot):
        return pltpu.make_async_copy(sums.at[spot], out.at[jnp.maximum(res_from[spot], 0)], sems.at[spot])

    for _, _, spot in spots:
        pl.when(res_first[spot] == spot)(write(spot).start)
    for _, _, spot in spots:
        pl.when(res_first[spot] == spot)(write(spot).wait)


def local(
    tasks,
    task_count,
    integrals,
    amplitudes,
    amp_slot,
    need_amp,
    res_slot,
    needed_residual_tiles,
    pair_energy,
    virt_energy,
    window_energy,
):
    owners = lax.axis_size("tile")
    me = lax.axis_index("tile").astype(jnp.int32)
    per_amp, _, row_count = amplitudes.shape
    per_res = res_slot.shape[0] // owners
    list_length = need_amp.shape[0]
    tile_count = virt_energy.shape[0] // TW
    slots = list_length * list_length
    task_slots = tasks.shape[1]

    amplitudes = pltpu.with_memory_space_constraint(amplitudes, pltpu.HBM)
    integrals = pltpu.with_memory_space_constraint(integrals, pltpu.HBM)
    amp_slot = pltpu.with_memory_space_constraint(amp_slot, pltpu.HBM)
    own_lists = jnp.concatenate([need_amp, needed_residual_tiles])
    spots = jnp.arange(owners, dtype=jnp.int32)[:, None] == me
    lists = lax.psum(jnp.where(spots, own_lists[None, :], 0), "tile").reshape(-1)
    me_ref = me.reshape(1)

    def exchange(buffers):
        return [
            in_vmem(lax.ppermute(buffers[d - 1], "tile", [(i, i ^ d) for i in range(owners)]))
            for d in class_order(owners)
        ]

    piece = pltpu.VMEM((CAP, TW, row_count), F32)
    packed = pl.pallas_call(
        functools.partial(pack_kernel, owners, per_amp),
        out_shape=[piece] * (owners - 1),
        in_specs=[SMEM_SPEC] * 3 + [HBM_SPEC],
        out_specs=[VMEM_SPEC] * (owners - 1),
        scratch_shapes=[
            pltpu.SMEM((owners * CAP + 1,), jnp.int32),
            pltpu.SemaphoreType.DMA((owners * CAP,)),
        ],
        compiler_params=params(),
        cost_estimate=cost(0, 2 * list_length * TW * row_count * 4),
        name="pack_tiles",
    )(me_ref, lists, amp_slot, amplitudes)
    fetched = exchange(packed)

    virt = in_vmem(jnp.broadcast_to(virt_energy.reshape(tile_count, TW, 1), (tile_count, TW, 128)))
    pair = in_vmem(pair_energy.reshape(1, row_count))
    small = pltpu.SMEM((owners * CAP + 1,), jnp.int32)
    *maps, inverse = pl.pallas_call(
        functools.partial(maps_kernel, owners, per_amp, per_res),
        out_shape=[small, pltpu.SMEM((CAP + 1,), jnp.int32), small, small, small]
        + [pltpu.VMEM((owners * CAP, TW, row_count), F32)],
        in_specs=[SMEM_SPEC] * 5 + [VMEM_SPEC] * 2,
        out_specs=[SMEM_SPEC] * 5 + [VMEM_SPEC],
        scratch_shapes=[
            pltpu.SMEM((owners * CAP + 1,), jnp.int32),
            pltpu.SMEM((owners,), jnp.int32),
            pltpu.SMEM((per_res + 1,), jnp.int32),
        ],
        compiler_params=params(),
        cost_estimate=cost(0, owners * CAP * TW * row_count * 4),
        name="list_maps",
    )(me_ref, lists, amp_slot, res_slot, window_energy, pair, virt)
    amp_from, amp_self, res_to, res_from, res_first = (
        pltpu.with_memory_space_constraint(x, pltpu.SMEM) for x in maps
    )
    inverse = in_vmem(inverse)
    block = 1024
    steps = TW * TW // block
    depth = list_length * TW
    operator_rows = depth // steps
    blank_rows = per_res * TW // steps
    keep = depth <= 1024
    operator = pltpu.VMEM((depth, depth), BF16) if keep else jax.ShapeDtypeStruct((depth, depth), BF16)
    operator_high, operator_low, blank = pl.pallas_call(
        functools.partial(sum_kernel, list_length),
        grid=(steps,),
        out_shape=[operator, operator, jax.ShapeDtypeStruct((per_res * TW, row_count), F32)],
        in_specs=[
            SMEM_SPEC,
            pl.BlockSpec((2, task_slots), lambda i: (0, 0)),
            pl.BlockSpec((task_slots, block), lambda i: (0, i)),
        ],
        out_specs=[
            pl.BlockSpec((operator_rows, depth), lambda i: (i, 0)),
            pl.BlockSpec((operator_rows, depth), lambda i: (i, 0)),
            pl.BlockSpec((blank_rows, row_count), lambda i: (i, 0)),
        ],
        scratch_shapes=[
            pltpu.VMEM((slots, task_slots), BF16),
            pltpu.VMEM((block // (2 * TW), slots, 2 * TW), F32),
            pltpu.VMEM((operator_rows, depth), F32),
        ],
        compiler_params=params(),
        cost_estimate=cost(4 * slots * task_slots * TW * TW, (task_slots + slots) * TW * TW * 4),
        name="sum_integrals",
    )(task_count, tasks, integrals)

    blank = blank.reshape(per_res, TW, row_count)
    if keep:
        operator_high, operator_low = in_vmem(operator_high), in_vmem(operator_low)
    products = pl.pallas_call(
        functools.partial(product_kernel, owners),
        out_shape=[piece] * owners,
        in_specs=[SMEM_SPEC] * 3 + [VMEM_SPEC] * 2 + [HBM_SPEC] + [VMEM_SPEC] * (owners - 1),
        out_specs=[VMEM_SPEC] * owners,
        scratch_shapes=[
            pltpu.VMEM((CAP, TW, row_count), F32),
            pltpu.VMEM((depth, row_count), BF16),
            pltpu.VMEM((depth, row_count), BF16),
            pltpu.VMEM((row_count // 128, depth, 128), F32),
            pltpu.SemaphoreType.DMA((CAP,)),
        ],
        compiler_params=params(),
        cost_estimate=cost(6 * depth * depth * row_count, 4 * depth * (depth + 2 * row_count)),
        name="multiply_tiles",
    )(amp_from, amp_self, res_to, operator_high, operator_low, amplitudes, *fetched)
    returned = [in_vmem(products[0])] + exchange(products[1:])
    return pl.pallas_call(
        functools.partial(final_kernel, owners),
        out_shape=jax.ShapeDtypeStruct((per_res, TW, row_count), F32),
        in_specs=[SMEM_SPEC] * 2 + [VMEM_SPEC] * (1 + owners) + [HBM_SPEC],
        out_specs=HBM_SPEC,
        scratch_shapes=[
            pltpu.VMEM((owners * CAP, TW, row_count), F32),
            pltpu.SemaphoreType.DMA((owners * CAP,)),
        ],
        input_output_aliases={3 + owners: 0},
        compiler_params=params(),
        cost_estimate=cost(0, per_res * TW * row_count * 4),
        name="finish_tiles",
    )(res_from, res_first, inverse, *returned, blank)


def solution(mesh):
    in_specs = (
        P(None, ("mol", "tile")),
        P(("mol", "tile")),
        P(("mol", "tile"), None),
        P(("mol", "tile"), None, "rep"),
        P("mol"),
        P(("mol", "tile")),
        P("mol"),
        P(("mol", "tile")),
        P(("mol", "rep")),
        P("mol"),
        P("mol"),
    )
    out_specs = P(("mol", "tile"), None, "rep")
    return jax.shard_map(local, mesh=mesh, in_specs=in_specs, out_specs=out_specs, check_vma=False)
```

```python
import functools

import jax
import jax.numpy as jnp
from jax import lax
from jax.experimental import pallas as pl
from jax.experimental.pallas import tpu as pltpu
from jax.sharding import PartitionSpec as P

TW = 64
CAP = 2
VMEM_LIMIT = 32 * 1024 * 1024
F32 = jnp.float32
BF16 = jnp.bfloat16

HBM_SPEC = pl.BlockSpec(memory_space=pl.ANY)
SMEM_SPEC = pl.BlockSpec(memory_space=pltpu.SMEM)
VMEM_SPEC = pl.BlockSpec(memory_space=pltpu.VMEM)


def class_order(owners):
    half = owners // 2
    far = [owners - 2, *range(half, owners - 2), owners - 1]
    near = [*range(2, half), 1]
    return [d for pair in zip(far, near) for d in pair] + far[len(near) :]


def params(limit=VMEM_LIMIT):
    return pltpu.CompilerParams(vmem_limit_bytes=limit)


def cost(flops, touched):
    return pl.CostEstimate(flops=flops, bytes_accessed=touched, transcendentals=0)


def in_vmem(array):
    return pltpu.with_memory_space_constraint(array, pltpu.VMEM)


def clear(ref, count, value):
    @pl.loop(0, count)
    def _(i):
        ref[i] = value


def pack_kernel(classes, list_length, per_owner, me_ref, lists_ref, amp_slot_ref, amplitudes, *rest):
    outs, (picked, sems) = rest[: len(classes)], rest[-2:]
    spare = len(classes) * CAP
    me = me_ref[0]
    low = me * per_owner
    clear(picked, spare, -1)

    def copy(at, k):
        local = picked[at * CAP + k]
        source = amplitudes.at[jnp.maximum(local, 0)]
        return local, pltpu.make_async_copy(source, outs[at].at[k], sems.at[at * CAP + k])

    for at, d in enumerate(classes):
        first = jnp.bitwise_xor(me, d) * 2 * list_length

        def note(j, count):
            local = amp_slot_ref[lists_ref[first + j]] - low
            mine = (local >= 0) & (local < per_owner)
            picked[jnp.where(mine, at * CAP + count, spare)] = local
            return count + mine.astype(jnp.int32)

        lax.fori_loop(0, list_length, note, jnp.int32(0), unroll=8)
        for k in range(CAP):
            local, moved = copy(at, k)
            pl.when(local >= 0)(moved.start)
    for at in range(len(classes)):
        for k in range(CAP):
            local, moved = copy(at, k)
            pl.when(local >= 0)(moved.wait)


def maps_kernel(
    owners, per_amp, per_res, me_ref, lists_ref, amp_slot_ref, res_slot_ref,
    window, pair, virt, amp_from, amp_self, res_to, res_from, res_first, inverse, res_tile, seen, taken,
):
    list_length = lists_ref.shape[0] // owners // 2
    spots = owners * CAP
    me = me_ref[0]
    for ref in (amp_from, res_to, res_from):
        clear(ref, spots, -1)
    clear(amp_self, CAP + 1, 0)
    clear(res_tile, spots, 0)
    clear(taken, per_res + 1, -1)

    def own_list(offset, slot_map, per_owner, place, self_slots):
        clear(seen, owners, 0)

        def note(g, carry):
            slot = slot_map[lists_ref[me * 2 * list_length + offset + g]]
            owner = lax.div(slot, jnp.int32(per_owner))
            d = jnp.bitwise_xor(owner, me)
            count = seen[d]
            place[d * CAP + count] = g
            seen[d] = count + 1
            if self_slots is not None:
                self_slots[jnp.where(d == 0, count, CAP)] = slot - owner * per_owner
            return carry

        lax.fori_loop(0, list_length, note, 0, unroll=8)

    own_list(0, amp_slot_ref, per_amp, amp_from, amp_self)
    own_list(list_length, res_slot_ref, per_res, res_to, None)
    low = me * per_res

    @pl.loop(0, owners)
    def _(partner):
        d = jnp.bitwise_xor(partner, me)

        def note(j, count):
            tile = lists_ref[partner * 2 * list_length + list_length + j]
            local = res_slot_ref[tile] - low
            mine = (local >= 0) & (local < per_res)
            spot = jnp.where(mine, d * CAP + count, spots)
            res_from[spot] = local
            res_tile[spot] = tile
            return count + mine.astype(jnp.int32)

        lax.fori_loop(0, list_length, note, jnp.int32(0), unroll=8)

    for d in [0] + class_order(owners):
        for spot in range(d * CAP, d * CAP + CAP):
            local = res_from[spot]
            at = jnp.where(local >= 0, local, per_res)
            first = jnp.where(local < 0, -1, jnp.where(taken[at] < 0, spot, taken[at]))
            taken[at] = first
            res_first[spot] = first

    tiles, columns = virt.shape[0], pair.shape[1]

    @pl.loop(0, spots)
    def _(spot):
        @pl.when(res_from[spot] >= 0)
        def _():
            tile = res_tile[spot]
            base = pair[...] - window[lax.div(tile, jnp.int32(tiles))]
            column = virt[lax.rem(tile, jnp.int32(tiles))]
            inverse[spot] = 1.0 / (base - jnp.concatenate([column] * (columns // 128), axis=1))


def sum_kernel(list_length, count_ref, tasks_ref, integrals_ref, high_ref, low_ref, blank_ref, hits, sums, matrix):
    slots = list_length * list_length
    tasks_here, block = integrals_ref.shape

    @pl.when(pl.program_id(0) == 0)
    def _():
        pair = tasks_ref[0:1, :] * list_length + tasks_ref[1:2, :]
        spot = lax.broadcasted_iota(jnp.int32, (1, tasks_here), 1)
        pair = jnp.where(spot < count_ref[0], pair, -1)
        row = lax.broadcasted_iota(jnp.int32, (slots, tasks_here), 0)
        hits[...] = jnp.where(row == pair, 1.0, 0.0).astype(BF16)

    blank_ref[...] = jnp.zeros_like(blank_ref)
    rows = integrals_ref[...]
    high = rows.astype(BF16)
    low = (rows - high.astype(F32)).astype(BF16)
    found = jnp.dot(hits[...], high, preferred_element_type=F32) + jnp.dot(
        hits[...], low, preferred_element_type=F32
    )
    for i in range(0, block // TW, 2):
        sums[i // 2] = found[:, i * TW : (i + 2) * TW]
    left = lax.broadcasted_iota(jnp.int32, (list_length, 2 * TW), 1) < TW
    for i in range(0, block // TW, 2):
        for a in range(0, list_length, 2):
            even = sums[i // 2, pl.ds(a, list_length, stride=list_length), :]
            odd = sums[i // 2, pl.ds(a + 1, list_length, stride=list_length), :]
            lanes = pl.ds(a * TW, 2 * TW)
            matrix[pl.ds(i * list_length, list_length), lanes] = jnp.where(left, even, pltpu.roll(odd, TW, 1))
            matrix[pl.ds((i + 1) * list_length, list_length), lanes] = jnp.where(left, pltpu.roll(even, TW, 1), odd)
    whole = matrix[...]
    top = whole.astype(BF16)
    high_ref[...] = top
    low_ref[...] = (whole - top.astype(F32)).astype(BF16)


def product_kernel(owners, amp_from, amp_self, res_to, operator_high, operator_low, amplitudes, *rest):
    arrived, outs = dict(zip(class_order(owners), rest[: owners - 1])), rest[owners - 1 : 2 * owners - 1]
    own, high, low, totals, sems = rest[2 * owners - 1 :]
    rows, columns = high.shape

    def fetch(k):
        source = amplitudes.at[amp_self[k]]
        return pltpu.make_async_copy(source, own.at[k], sems.at[k])

    def split(d, k):
        g = amp_from[d * CAP + k]

        @pl.when(g >= 0)
        def _():
            if d == 0:
                fetch(k).wait()
                values = own[k]
            else:
                values = arrived[d][k]
            top = values.astype(BF16)
            spot = pl.ds(pl.multiple_of(g * TW, TW), TW)
            high[spot, :] = top
            low[spot, :] = (values - top.astype(F32)).astype(BF16)

    for k in range(CAP):
        pl.when(amp_from[k] >= 0)(fetch(k).start)
    for d in range(owners - 1, -1, -1):
        for k in range(CAP):
            split(d, k)
    step = min(rows, 8 * TW)

    @pl.loop(0, rows // step)
    def _(i):
        here = pl.ds(pl.multiple_of(i * step, step), step)
        total = jnp.dot(operator_high[here, :], low[...], preferred_element_type=F32)
        total += jnp.dot(operator_low[here, :], high[...], preferred_element_type=F32)
        total += jnp.dot(operator_high[here, :], high[...], preferred_element_type=F32)
        for c in range(columns // 128):
            totals[c, here, :] = total[:, c * 128 : (c + 1) * 128]

    for d in range(owners):
        for k in range(CAP):
            g = res_to[d * CAP + k]

            @pl.when(g >= 0)
            def _():
                for c in range(columns // 128):
                    outs[d][k, :, c * 128 : (c + 1) * 128] = totals[c, pl.ds(g, TW, stride=rows // TW), :]


def final_kernel(owners, res_from, res_first, inverse, *rest):
    arrived, (_, out, sums, sems) = rest[:owners], rest[-4:]
    spots = [(at, k, d * CAP + k) for at, d in enumerate([0] + class_order(owners)) for k in range(CAP)]
    for at, k, spot in spots:
        first = res_first[spot]

        @pl.when(first == spot)
        def _():
            sums[spot] = arrived[at][k] * inverse[spot]

        @pl.when((first >= 0) & (first != spot))
        def _():
            sums[first] = sums[first] + arrived[at][k] * inverse[spot]

    def write(spot):
        return pltpu.make_async_copy(sums.at[spot], out.at[jnp.maximum(res_from[spot], 0)], sems.at[spot])

    for _, _, spot in spots:
        pl.when(res_first[spot] == spot)(write(spot).start)
    for _, _, spot in spots:
        pl.when(res_first[spot] == spot)(write(spot).wait)


def local(
    tasks,
    task_count,
    integrals,
    amplitudes,
    amp_slot,
    need_amp,
    res_slot,
    needed_residual_tiles,
    pair_energy,
    virt_energy,
    window_energy,
):
    owners = lax.axis_size("tile")
    me = lax.axis_index("tile").astype(jnp.int32)
    per_amp, _, row_count = amplitudes.shape
    per_res = res_slot.shape[0] // owners
    list_length = need_amp.shape[0]
    tile_count = virt_energy.shape[0] // TW
    slots = list_length * list_length
    task_slots = tasks.shape[1]

    amplitudes = pltpu.with_memory_space_constraint(amplitudes, pltpu.HBM)
    integrals = pltpu.with_memory_space_constraint(integrals, pltpu.HBM)
    amp_slot = pltpu.with_memory_space_constraint(amp_slot, pltpu.HBM)
    own_lists = jnp.concatenate([need_amp, needed_residual_tiles])
    spots = jnp.arange(owners, dtype=jnp.int32)[:, None] == me
    lists = lax.psum(jnp.where(spots, own_lists[None, :], 0), "tile").reshape(-1)
    me_ref = me.reshape(1)

    order = class_order(owners)

    def exchange(buffers, classes):
        return [
            in_vmem(lax.ppermute(buffer, "tile", [(i, i ^ d) for i in range(owners)]))
            for buffer, d in zip(buffers, classes)
        ]

    piece = pltpu.VMEM((CAP, TW, row_count), F32)
    fetched = []
    for classes in order[:1], order[1:]:
        packed = pl.pallas_call(
            functools.partial(pack_kernel, classes, list_length, per_amp),
            out_shape=[piece] * len(classes),
            in_specs=[SMEM_SPEC] * 3 + [HBM_SPEC],
            out_specs=[VMEM_SPEC] * len(classes),
            scratch_shapes=[
                pltpu.SMEM((len(classes) * CAP + 1,), jnp.int32),
                pltpu.SemaphoreType.DMA((len(classes) * CAP,)),
            ],
            compiler_params=params(),
            cost_estimate=cost(0, len(classes) * CAP * TW * row_count * 4),
            name="pack_tiles",
        )(me_ref, lists, amp_slot, amplitudes)
        fetched += exchange(packed, classes)

    virt = in_vmem(jnp.broadcast_to(virt_energy.reshape(tile_count, TW, 1), (tile_count, TW, 128)))
    pair = in_vmem(pair_energy.reshape(1, row_count))
    small = pltpu.SMEM((owners * CAP + 1,), jnp.int32)
    *maps, inverse = pl.pallas_call(
        functools.partial(maps_kernel, owners, per_amp, per_res),
        out_shape=[small, pltpu.SMEM((CAP + 1,), jnp.int32), small, small, small]
        + [pltpu.VMEM((owners * CAP, TW, row_count), F32)],
        in_specs=[SMEM_SPEC] * 5 + [VMEM_SPEC] * 2,
        out_specs=[SMEM_SPEC] * 5 + [VMEM_SPEC],
        scratch_shapes=[
            pltpu.SMEM((owners * CAP + 1,), jnp.int32),
            pltpu.SMEM((owners,), jnp.int32),
            pltpu.SMEM((per_res + 1,), jnp.int32),
        ],
        compiler_params=params(),
        cost_estimate=cost(0, owners * CAP * TW * row_count * 4),
        name="list_maps",
    )(me_ref, lists, amp_slot, res_slot, window_energy, pair, virt)
    amp_from, amp_self, res_to, res_from, res_first = (
        pltpu.with_memory_space_constraint(x, pltpu.SMEM) for x in maps
    )
    inverse = in_vmem(inverse)
    block = 1024
    steps = TW * TW // block
    depth = list_length * TW
    operator_rows = depth // steps
    blank_rows = per_res * TW // steps
    keep = depth <= 1024
    operator = pltpu.VMEM((depth, depth), BF16) if keep else jax.ShapeDtypeStruct((depth, depth), BF16)
    operator_high, operator_low, blank = pl.pallas_call(
        functools.partial(sum_kernel, list_length),
        grid=(steps,),
        out_shape=[operator, operator, jax.ShapeDtypeStruct((per_res * TW, row_count), F32)],
        in_specs=[
            SMEM_SPEC,
            pl.BlockSpec((2, task_slots), lambda i: (0, 0)),
            pl.BlockSpec((task_slots, block), lambda i: (0, i)),
        ],
        out_specs=[
            pl.BlockSpec((operator_rows, depth), lambda i: (i, 0)),
            pl.BlockSpec((operator_rows, depth), lambda i: (i, 0)),
            pl.BlockSpec((blank_rows, row_count), lambda i: (i, 0)),
        ],
        scratch_shapes=[
            pltpu.VMEM((slots, task_slots), BF16),
            pltpu.VMEM((block // (2 * TW), slots, 2 * TW), F32),
            pltpu.VMEM((operator_rows, depth), F32),
        ],
        compiler_params=params(),
        cost_estimate=cost(4 * slots * task_slots * TW * TW, (task_slots + slots) * TW * TW * 4),
        name="sum_integrals",
    )(task_count, tasks, integrals)

    blank = blank.reshape(per_res, TW, row_count)
    if keep:
        operator_high, operator_low = in_vmem(operator_high), in_vmem(operator_low)
    products = pl.pallas_call(
        functools.partial(product_kernel, owners),
        out_shape=[piece] * owners,
        in_specs=[SMEM_SPEC] * 3 + [VMEM_SPEC] * 2 + [HBM_SPEC] + [VMEM_SPEC] * (owners - 1),
        out_specs=[VMEM_SPEC] * owners,
        scratch_shapes=[
            pltpu.VMEM((CAP, TW, row_count), F32),
            pltpu.VMEM((depth, row_count), BF16),
            pltpu.VMEM((depth, row_count), BF16),
            pltpu.VMEM((row_count // 128, depth, 128), F32),
            pltpu.SemaphoreType.DMA((CAP,)),
        ],
        compiler_params=params(),
        cost_estimate=cost(6 * depth * depth * row_count, 4 * depth * (depth + 2 * row_count)),
        name="multiply_tiles",
    )(amp_from, amp_self, res_to, operator_high, operator_low, amplitudes, *fetched)
    returned = [in_vmem(products[0])] + exchange([products[d] for d in order], order)
    return pl.pallas_call(
        functools.partial(final_kernel, owners),
        out_shape=jax.ShapeDtypeStruct((per_res, TW, row_count), F32),
        in_specs=[SMEM_SPEC] * 2 + [VMEM_SPEC] * (1 + owners) + [HBM_SPEC],
        out_specs=HBM_SPEC,
        scratch_shapes=[
            pltpu.VMEM((owners * CAP, TW, row_count), F32),
            pltpu.SemaphoreType.DMA((owners * CAP,)),
        ],
        input_output_aliases={3 + owners: 0},
        compiler_params=params(),
        cost_estimate=cost(0, per_res * TW * row_count * 4),
        name="finish_tiles",
    )(res_from, res_first, inverse, *returned, blank)


def solution(mesh):
    in_specs = (
        P(None, ("mol", "tile")),
        P(("mol", "tile")),
        P(("mol", "tile"), None),
        P(("mol", "tile"), None, "rep"),
        P("mol"),
        P(("mol", "tile")),
        P("mol"),
        P(("mol", "tile")),
        P(("mol", "rep")),
        P("mol"),
        P("mol"),
    )
    out_specs = P(("mol", "tile"), None, "rep")
    return jax.shard_map(local, mesh=mesh, in_specs=in_specs, out_specs=out_specs, check_vma=False)
```

```python
import functools

import jax
import jax.numpy as jnp
from jax import lax
from jax.experimental import pallas as pl
from jax.experimental.pallas import tpu as pltpu
from jax.sharding import PartitionSpec as P

TW = 64
CAP = 2
VMEM_LIMIT = 32 * 1024 * 1024
F32 = jnp.float32
BF16 = jnp.bfloat16

HBM_SPEC = pl.BlockSpec(memory_space=pl.ANY)
SMEM_SPEC = pl.BlockSpec(memory_space=pltpu.SMEM)
VMEM_SPEC = pl.BlockSpec(memory_space=pltpu.VMEM)


def class_order(owners):
    half = owners // 2
    far = [owners - 2, *range(half, owners - 2), owners - 1]
    near = [*range(2, half), 1]
    return [d for pair in zip(far, near) for d in pair] + far[len(near) :]


def params(limit=VMEM_LIMIT):
    return pltpu.CompilerParams(vmem_limit_bytes=limit)


def cost(flops, touched):
    return pl.CostEstimate(flops=flops, bytes_accessed=touched, transcendentals=0)


def in_vmem(array):
    return pltpu.with_memory_space_constraint(array, pltpu.VMEM)


def clear(ref, count, value):
    @pl.loop(0, count)
    def _(i):
        ref[i] = value


def spread_kernel(list_length, me_ref, need_ref, needed_ref, amp_slot_ref, spread):
    shape = spread.shape
    at = lax.broadcasted_iota(jnp.int32, shape, 0) * shape[1] + lax.broadcasted_iota(jnp.int32, shape, 1)
    at = at - me_ref[0] * 2 * list_length
    values = jnp.zeros(shape, jnp.int32)
    for j in range(list_length):
        values = jnp.where(at == j, amp_slot_ref[need_ref[j]], values)
        values = jnp.where(at == list_length + j, needed_ref[j], values)
    spread[...] = values


def pack_kernel(classes, list_length, per_owner, me_ref, lists_ref, amplitudes, *rest):
    outs, (picked, sems) = rest[: len(classes)], rest[-2:]
    spare = len(classes) * CAP
    me = me_ref[0]
    low = me * per_owner
    clear(picked, spare, -1)

    def copy(at, k):
        local = picked[at * CAP + k]
        source = amplitudes.at[jnp.maximum(local, 0)]
        return local, pltpu.make_async_copy(source, outs[at].at[k], sems.at[at * CAP + k])

    for at, d in enumerate(classes):
        first = jnp.bitwise_xor(me, d) * 2 * list_length

        def note(j, count):
            local = lists_ref[first + j] - low
            mine = (local >= 0) & (local < per_owner)
            picked[jnp.where(mine, at * CAP + count, spare)] = local
            return count + mine.astype(jnp.int32)

        lax.fori_loop(0, list_length, note, jnp.int32(0), unroll=8)
        for k in range(CAP):
            local, moved = copy(at, k)
            pl.when(local >= 0)(moved.start)
    for at in range(len(classes)):
        for k in range(CAP):
            local, moved = copy(at, k)
            pl.when(local >= 0)(moved.wait)


def maps_kernel(
    owners, per_amp, per_res, me_ref, lists_ref, res_slot_ref,
    window, pair, virt, amp_from, amp_self, res_to, res_from, res_first, inverse, res_tile, seen, taken,
):
    list_length = lists_ref.shape[0] // owners // 2
    spots = owners * CAP
    me = me_ref[0]
    for ref in (amp_from, res_to, res_from):
        clear(ref, spots, -1)
    clear(amp_self, CAP + 1, 0)
    clear(res_tile, spots, 0)
    clear(taken, per_res + 1, -1)

    def own_list(offset, slot_map, per_owner, place, self_slots):
        clear(seen, owners, 0)

        def note(g, carry):
            slot = lists_ref[me * 2 * list_length + offset + g]
            if slot_map is not None:
                slot = slot_map[slot]
            owner = lax.div(slot, jnp.int32(per_owner))
            d = jnp.bitwise_xor(owner, me)
            count = seen[d]
            place[d * CAP + count] = g
            seen[d] = count + 1
            if self_slots is not None:
                self_slots[jnp.where(d == 0, count, CAP)] = slot - owner * per_owner
            return carry

        lax.fori_loop(0, list_length, note, 0, unroll=8)

    own_list(0, None, per_amp, amp_from, amp_self)
    own_list(list_length, res_slot_ref, per_res, res_to, None)
    low = me * per_res

    @pl.loop(0, owners)
    def _(partner):
        d = jnp.bitwise_xor(partner, me)

        def note(j, count):
            tile = lists_ref[partner * 2 * list_length + list_length + j]
            local = res_slot_ref[tile] - low
            mine = (local >= 0) & (local < per_res)
            spot = jnp.where(mine, d * CAP + count, spots)
            res_from[spot] = local
            res_tile[spot] = tile
            return count + mine.astype(jnp.int32)

        lax.fori_loop(0, list_length, note, jnp.int32(0), unroll=8)

    for d in [0] + class_order(owners):
        for spot in range(d * CAP, d * CAP + CAP):
            local = res_from[spot]
            at = jnp.where(local >= 0, local, per_res)
            first = jnp.where(local < 0, -1, jnp.where(taken[at] < 0, spot, taken[at]))
            taken[at] = first
            res_first[spot] = first

    tiles, columns = virt.shape[0], pair.shape[1]

    @pl.loop(0, spots)
    def _(spot):
        @pl.when(res_from[spot] >= 0)
        def _():
            tile = res_tile[spot]
            base = pair[...] - window[lax.div(tile, jnp.int32(tiles))]
            column = virt[lax.rem(tile, jnp.int32(tiles))]
            inverse[spot] = 1.0 / (base - jnp.concatenate([column] * (columns // 128), axis=1))


def sum_kernel(list_length, count_ref, tasks_ref, integrals_ref, high_ref, low_ref, blank_ref, hits, sums, matrix):
    slots = list_length * list_length
    tasks_here, block = integrals_ref.shape

    @pl.when(pl.program_id(0) == 0)
    def _():
        pair = tasks_ref[0:1, :] * list_length + tasks_ref[1:2, :]
        spot = lax.broadcasted_iota(jnp.int32, (1, tasks_here), 1)
        pair = jnp.where(spot < count_ref[0], pair, -1)
        row = lax.broadcasted_iota(jnp.int32, (slots, tasks_here), 0)
        hits[...] = jnp.where(row == pair, 1.0, 0.0).astype(BF16)

    blank_ref[...] = jnp.zeros_like(blank_ref)
    rows = integrals_ref[...]
    high = rows.astype(BF16)
    low = (rows - high.astype(F32)).astype(BF16)
    found = jnp.dot(hits[...], high, preferred_element_type=F32) + jnp.dot(
        hits[...], low, preferred_element_type=F32
    )
    for i in range(0, block // TW, 2):
        sums[i // 2] = found[:, i * TW : (i + 2) * TW]
    left = lax.broadcasted_iota(jnp.int32, (list_length, 2 * TW), 1) < TW
    for i in range(0, block // TW, 2):
        for a in range(0, list_length, 2):
            even = sums[i // 2, pl.ds(a, list_length, stride=list_length), :]
            odd = sums[i // 2, pl.ds(a + 1, list_length, stride=list_length), :]
            lanes = pl.ds(a * TW, 2 * TW)
            matrix[pl.ds(i * list_length, list_length), lanes] = jnp.where(left, even, pltpu.roll(odd, TW, 1))
            matrix[pl.ds((i + 1) * list_length, list_length), lanes] = jnp.where(left, pltpu.roll(even, TW, 1), odd)
    whole = matrix[...]
    top = whole.astype(BF16)
    high_ref[...] = top
    low_ref[...] = (whole - top.astype(F32)).astype(BF16)


def product_kernel(owners, amp_from, amp_self, res_to, operator_high, operator_low, amplitudes, *rest):
    arrived, outs = dict(zip(class_order(owners), rest[: owners - 1])), rest[owners - 1 : 2 * owners - 1]
    own, high, low, totals, sems = rest[2 * owners - 1 :]
    rows, columns = high.shape

    def fetch(k):
        source = amplitudes.at[amp_self[k]]
        return pltpu.make_async_copy(source, own.at[k], sems.at[k])

    def split(d, k):
        g = amp_from[d * CAP + k]

        @pl.when(g >= 0)
        def _():
            if d == 0:
                fetch(k).wait()
                values = own[k]
            else:
                values = arrived[d][k]
            top = values.astype(BF16)
            spot = pl.ds(pl.multiple_of(g * TW, TW), TW)
            high[spot, :] = top
            low[spot, :] = (values - top.astype(F32)).astype(BF16)

    for k in range(CAP):
        pl.when(amp_from[k] >= 0)(fetch(k).start)
    for d in range(owners - 1, -1, -1):
        for k in range(CAP):
            split(d, k)
    step = min(rows, 8 * TW)

    @pl.loop(0, rows // step)
    def _(i):
        here = pl.ds(pl.multiple_of(i * step, step), step)
        total = jnp.dot(operator_high[here, :], low[...], preferred_element_type=F32)
        total += jnp.dot(operator_low[here, :], high[...], preferred_element_type=F32)
        total += jnp.dot(operator_high[here, :], high[...], preferred_element_type=F32)
        for c in range(columns // 128):
            totals[c, here, :] = total[:, c * 128 : (c + 1) * 128]

    for d in range(owners):
        for k in range(CAP):
            g = res_to[d * CAP + k]

            @pl.when(g >= 0)
            def _():
                for c in range(columns // 128):
                    outs[d][k, :, c * 128 : (c + 1) * 128] = totals[c, pl.ds(g, TW, stride=rows // TW), :]


def final_kernel(owners, res_from, res_first, inverse, *rest):
    arrived, (_, out, sums, sems) = rest[:owners], rest[-4:]
    spots = [(at, k, d * CAP + k) for at, d in enumerate([0] + class_order(owners)) for k in range(CAP)]
    for at, k, spot in spots:
        first = res_first[spot]

        @pl.when(first == spot)
        def _():
            sums[spot] = arrived[at][k] * inverse[spot]

        @pl.when((first >= 0) & (first != spot))
        def _():
            sums[first] = sums[first] + arrived[at][k] * inverse[spot]

    def write(spot):
        return pltpu.make_async_copy(sums.at[spot], out.at[jnp.maximum(res_from[spot], 0)], sems.at[spot])

    for _, _, spot in spots:
        pl.when(res_first[spot] == spot)(write(spot).start)
    for _, _, spot in spots:
        pl.when(res_first[spot] == spot)(write(spot).wait)


def local(
    tasks,
    task_count,
    integrals,
    amplitudes,
    amp_slot,
    need_amp,
    res_slot,
    needed_residual_tiles,
    pair_energy,
    virt_energy,
    window_energy,
):
    owners = lax.axis_size("tile")
    me = lax.axis_index("tile").astype(jnp.int32)
    per_amp, _, row_count = amplitudes.shape
    per_res = res_slot.shape[0] // owners
    list_length = need_amp.shape[0]
    tile_count = virt_energy.shape[0] // TW
    slots = list_length * list_length
    task_slots = tasks.shape[1]

    amplitudes = pltpu.with_memory_space_constraint(amplitudes, pltpu.HBM)
    integrals = pltpu.with_memory_space_constraint(integrals, pltpu.HBM)
    me_ref = me.reshape(1)
    in_hbm = functools.partial(pltpu.with_memory_space_constraint, memory_space=pltpu.HBM)
    spread = pl.pallas_call(
        functools.partial(spread_kernel, list_length),
        out_shape=pltpu.VMEM((owners * 2 * list_length // 128, 128), jnp.int32),
        in_specs=[SMEM_SPEC] * 4,
        out_specs=VMEM_SPEC,
        compiler_params=params(),
        cost_estimate=cost(0, owners * 2 * list_length * 4),
        name="spread_lists",
    )(me_ref, in_hbm(need_amp), in_hbm(needed_residual_tiles), in_hbm(amp_slot))
    lists = lax.psum(spread, "tile").reshape(-1)
    order = class_order(owners)

    def exchange(buffers, classes):
        return [
            in_vmem(lax.ppermute(buffer, "tile", [(i, i ^ d) for i in range(owners)]))
            for buffer, d in zip(buffers, classes)
        ]

    piece = pltpu.VMEM((CAP, TW, row_count), F32)
    fetched = []
    for classes in order[:1], order[1:]:
        packed = pl.pallas_call(
            functools.partial(pack_kernel, classes, list_length, per_amp),
            out_shape=[piece] * len(classes),
            in_specs=[SMEM_SPEC] * 2 + [HBM_SPEC],
            out_specs=[VMEM_SPEC] * len(classes),
            scratch_shapes=[
                pltpu.SMEM((len(classes) * CAP + 1,), jnp.int32),
                pltpu.SemaphoreType.DMA((len(classes) * CAP,)),
            ],
            compiler_params=params(),
            cost_estimate=cost(0, len(classes) * CAP * TW * row_count * 4),
            name="pack_tiles",
        )(me_ref, lists, amplitudes)
        fetched += exchange(packed, classes)

    virt = in_vmem(jnp.broadcast_to(virt_energy.reshape(tile_count, TW, 1), (tile_count, TW, 128)))
    pair = in_vmem(pair_energy.reshape(1, row_count))
    small = pltpu.SMEM((owners * CAP + 1,), jnp.int32)
    *maps, inverse = pl.pallas_call(
        functools.partial(maps_kernel, owners, per_amp, per_res),
        out_shape=[small, pltpu.SMEM((CAP + 1,), jnp.int32), small, small, small]
        + [pltpu.VMEM((owners * CAP, TW, row_count), F32)],
        in_specs=[SMEM_SPEC] * 4 + [VMEM_SPEC] * 2,
        out_specs=[SMEM_SPEC] * 5 + [VMEM_SPEC],
        scratch_shapes=[
            pltpu.SMEM((owners * CAP + 1,), jnp.int32),
            pltpu.SMEM((owners,), jnp.int32),
            pltpu.SMEM((per_res + 1,), jnp.int32),
        ],
        compiler_params=params(),
        cost_estimate=cost(0, owners * CAP * TW * row_count * 4),
        name="list_maps",
    )(me_ref, lists, res_slot, window_energy, pair, virt)
    amp_from, amp_self, res_to, res_from, res_first = (
        pltpu.with_memory_space_constraint(x, pltpu.SMEM) for x in maps
    )
    inverse = in_vmem(inverse)
    block = 1024
    steps = TW * TW // block
    depth = list_length * TW
    operator_rows = depth // steps
    blank_rows = per_res * TW // steps
    keep = depth <= 1024
    operator = pltpu.VMEM((depth, depth), BF16) if keep else jax.ShapeDtypeStruct((depth, depth), BF16)
    operator_high, operator_low, blank = pl.pallas_call(
        functools.partial(sum_kernel, list_length),
        grid=(steps,),
        out_shape=[operator, operator, jax.ShapeDtypeStruct((per_res * TW, row_count), F32)],
        in_specs=[
            SMEM_SPEC,
            pl.BlockSpec((2, task_slots), lambda i: (0, 0)),
            pl.BlockSpec((task_slots, block), lambda i: (0, i)),
        ],
        out_specs=[
            pl.BlockSpec((operator_rows, depth), lambda i: (i, 0)),
            pl.BlockSpec((operator_rows, depth), lambda i: (i, 0)),
            pl.BlockSpec((blank_rows, row_count), lambda i: (i, 0)),
        ],
        scratch_shapes=[
            pltpu.VMEM((slots, task_slots), BF16),
            pltpu.VMEM((block // (2 * TW), slots, 2 * TW), F32),
            pltpu.VMEM((operator_rows, depth), F32),
        ],
        compiler_params=params(),
        cost_estimate=cost(4 * slots * task_slots * TW * TW, (task_slots + slots) * TW * TW * 4),
        name="sum_integrals",
    )(task_count, tasks, integrals)

    blank = blank.reshape(per_res, TW, row_count)
    if keep:
        operator_high, operator_low = in_vmem(operator_high), in_vmem(operator_low)
    products = pl.pallas_call(
        functools.partial(product_kernel, owners),
        out_shape=[piece] * owners,
        in_specs=[SMEM_SPEC] * 3 + [VMEM_SPEC] * 2 + [HBM_SPEC] + [VMEM_SPEC] * (owners - 1),
        out_specs=[VMEM_SPEC] * owners,
        scratch_shapes=[
            pltpu.VMEM((CAP, TW, row_count), F32),
            pltpu.VMEM((depth, row_count), BF16),
            pltpu.VMEM((depth, row_count), BF16),
            pltpu.VMEM((row_count // 128, depth, 128), F32),
            pltpu.SemaphoreType.DMA((CAP,)),
        ],
        compiler_params=params(),
        cost_estimate=cost(6 * depth * depth * row_count, 4 * depth * (depth + 2 * row_count)),
        name="multiply_tiles",
    )(amp_from, amp_self, res_to, operator_high, operator_low, amplitudes, *fetched)
    returned = [in_vmem(products[0])] + exchange([products[d] for d in order], order)
    return pl.pallas_call(
        functools.partial(final_kernel, owners),
        out_shape=jax.ShapeDtypeStruct((per_res, TW, row_count), F32),
        in_specs=[SMEM_SPEC] * 2 + [VMEM_SPEC] * (1 + owners) + [HBM_SPEC],
        out_specs=HBM_SPEC,
        scratch_shapes=[
            pltpu.VMEM((owners * CAP, TW, row_count), F32),
            pltpu.SemaphoreType.DMA((owners * CAP,)),
        ],
        input_output_aliases={3 + owners: 0},
        compiler_params=params(),
        cost_estimate=cost(0, per_res * TW * row_count * 4),
        name="finish_tiles",
    )(res_from, res_first, inverse, *returned, blank)


def solution(mesh):
    in_specs = (
        P(None, ("mol", "tile")),
        P(("mol", "tile")),
        P(("mol", "tile"), None),
        P(("mol", "tile"), None, "rep"),
        P("mol"),
        P(("mol", "tile")),
        P("mol"),
        P(("mol", "tile")),
        P(("mol", "rep")),
        P("mol"),
        P("mol"),
    )
    out_specs = P(("mol", "tile"), None, "rep")
    return jax.shard_map(local, mesh=mesh, in_specs=in_specs, out_specs=out_specs, check_vma=False)
```

```python
import functools

import jax
import jax.numpy as jnp
from jax import lax
from jax.experimental import pallas as pl
from jax.experimental.pallas import tpu as pltpu
from jax.sharding import PartitionSpec as P

TW = 64
CAP = 2
VMEM_LIMIT = 32 * 1024 * 1024
F32 = jnp.float32
BF16 = jnp.bfloat16

HBM_SPEC = pl.BlockSpec(memory_space=pl.ANY)
SMEM_SPEC = pl.BlockSpec(memory_space=pltpu.SMEM)
VMEM_SPEC = pl.BlockSpec(memory_space=pltpu.VMEM)


def class_order(owners):
    half = owners // 2
    far = [owners - 2, *range(half, owners - 2), owners - 1]
    near = [*range(2, half), 1]
    return [d for pair in zip(far, near) for d in pair] + far[len(near) :]


def params(limit=VMEM_LIMIT):
    return pltpu.CompilerParams(vmem_limit_bytes=limit)


def cost(flops, touched):
    return pl.CostEstimate(flops=flops, bytes_accessed=touched, transcendentals=0)


def in_vmem(array):
    return pltpu.with_memory_space_constraint(array, pltpu.VMEM)


def clear(ref, count, value):
    @pl.loop(0, count)
    def _(i):
        ref[i] = value


def spread_kernel(list_length, me_ref, need_ref, needed_ref, amp_slot_ref, spread):
    shape = spread.shape
    at = lax.broadcasted_iota(jnp.int32, shape, 0) * shape[1] + lax.broadcasted_iota(jnp.int32, shape, 1)
    at = at - me_ref[0] * 2 * list_length
    values = jnp.zeros(shape, jnp.int32)
    for j in range(list_length):
        values = jnp.where(at == j, amp_slot_ref[need_ref[j]], values)
        values = jnp.where(at == list_length + j, needed_ref[j], values)
    spread[...] = values


def pack_kernel(classes, list_length, per_owner, me_ref, lists_ref, amplitudes, *rest):
    outs, (picked, sems) = rest[: len(classes)], rest[-2:]
    spare = len(classes) * CAP
    me = me_ref[0]
    low = me * per_owner
    clear(picked, spare, -1)

    def copy(at, k):
        local = picked[at * CAP + k]
        source = amplitudes.at[jnp.maximum(local, 0)]
        return local, pltpu.make_async_copy(source, outs[at].at[k], sems.at[at * CAP + k])

    for at, d in enumerate(classes):
        first = jnp.bitwise_xor(me, d) * 2 * list_length

        def note(j, count):
            local = lists_ref[first + j] - low
            mine = (local >= 0) & (local < per_owner)
            picked[jnp.where(mine, at * CAP + count, spare)] = local
            return count + mine.astype(jnp.int32)

        lax.fori_loop(0, list_length, note, jnp.int32(0), unroll=8)
        for k in range(CAP):
            local, moved = copy(at, k)
            pl.when(local >= 0)(moved.start)
    for at in range(len(classes)):
        for k in range(CAP):
            local, moved = copy(at, k)
            pl.when(local >= 0)(moved.wait)


def maps_kernel(
    owners, per_amp, per_res, me_ref, lists_ref, res_slot_ref,
    window, pair, virt, amp_from, amp_self, res_to, res_from, res_first, res_last, inverse, res_tile, seen, taken,
):
    list_length = lists_ref.shape[0] // owners // 2
    spots = owners * CAP
    me = me_ref[0]
    for ref in (amp_from, res_to, res_from):
        clear(ref, spots, -1)
    clear(amp_self, CAP + 1, 0)
    clear(res_tile, spots, 0)
    clear(taken, per_res + 1, -1)

    def own_list(offset, slot_map, per_owner, place, self_slots):
        clear(seen, owners, 0)

        def note(g, carry):
            slot = lists_ref[me * 2 * list_length + offset + g]
            if slot_map is not None:
                slot = slot_map[slot]
            owner = lax.div(slot, jnp.int32(per_owner))
            d = jnp.bitwise_xor(owner, me)
            count = seen[d]
            place[d * CAP + count] = g
            seen[d] = count + 1
            if self_slots is not None:
                self_slots[jnp.where(d == 0, count, CAP)] = slot - owner * per_owner
            return carry

        lax.fori_loop(0, list_length, note, 0, unroll=8)

    own_list(0, None, per_amp, amp_from, amp_self)
    own_list(list_length, res_slot_ref, per_res, res_to, None)
    low = me * per_res

    @pl.loop(0, owners)
    def _(partner):
        d = jnp.bitwise_xor(partner, me)

        def note(j, count):
            tile = lists_ref[partner * 2 * list_length + list_length + j]
            local = res_slot_ref[tile] - low
            mine = (local >= 0) & (local < per_res)
            spot = jnp.where(mine, d * CAP + count, spots)
            res_from[spot] = local
            res_tile[spot] = tile
            return count + mine.astype(jnp.int32)

        lax.fori_loop(0, list_length, note, jnp.int32(0), unroll=8)

    for d in [0] + class_order(owners):
        for spot in range(d * CAP, d * CAP + CAP):
            local = res_from[spot]
            at = jnp.where(local >= 0, local, per_res)
            first = jnp.where(local < 0, -1, jnp.where(taken[at] < 0, spot, taken[at]))
            taken[at] = first
            res_first[spot] = first

    clear(taken, per_res + 1, -1)
    for d in reversed([0] + class_order(owners)):
        for spot in reversed(range(d * CAP, d * CAP + CAP)):
            local = res_from[spot]
            at = jnp.where(local >= 0, local, per_res)
            res_last[spot] = jnp.where((local >= 0) & (taken[at] < 0), 1, 0)
            taken[at] = jnp.where(local >= 0, spot, -1)

    tiles, columns = virt.shape[0], pair.shape[1]

    @pl.loop(0, spots)
    def _(spot):
        @pl.when(res_from[spot] >= 0)
        def _():
            tile = res_tile[spot]
            base = pair[...] - window[lax.div(tile, jnp.int32(tiles))]
            column = virt[lax.rem(tile, jnp.int32(tiles))]
            inverse[spot] = 1.0 / (base - jnp.concatenate([column] * (columns // 128), axis=1))


def sum_kernel(list_length, count_ref, tasks_ref, integrals_ref, high_ref, low_ref, blank_ref, hits, sums, matrix):
    slots = list_length * list_length
    tasks_here, block = integrals_ref.shape

    @pl.when(pl.program_id(0) == 0)
    def _():
        pair = tasks_ref[0:1, :] * list_length + tasks_ref[1:2, :]
        spot = lax.broadcasted_iota(jnp.int32, (1, tasks_here), 1)
        pair = jnp.where(spot < count_ref[0], pair, -1)
        row = lax.broadcasted_iota(jnp.int32, (slots, tasks_here), 0)
        hits[...] = jnp.where(row == pair, 1.0, 0.0).astype(BF16)

    blank_ref[...] = jnp.zeros_like(blank_ref)
    rows = integrals_ref[...]
    high = rows.astype(BF16)
    low = (rows - high.astype(F32)).astype(BF16)
    found = jnp.dot(hits[...], high, preferred_element_type=F32) + jnp.dot(
        hits[...], low, preferred_element_type=F32
    )
    for i in range(0, block // TW, 2):
        sums[i // 2] = found[:, i * TW : (i + 2) * TW]
    left = lax.broadcasted_iota(jnp.int32, (list_length, 2 * TW), 1) < TW
    for i in range(0, block // TW, 2):
        for a in range(0, list_length, 2):
            even = sums[i // 2, pl.ds(a, list_length, stride=list_length), :]
            odd = sums[i // 2, pl.ds(a + 1, list_length, stride=list_length), :]
            lanes = pl.ds(a * TW, 2 * TW)
            matrix[pl.ds(i * list_length, list_length), lanes] = jnp.where(left, even, pltpu.roll(odd, TW, 1))
            matrix[pl.ds((i + 1) * list_length, list_length), lanes] = jnp.where(left, pltpu.roll(even, TW, 1), odd)
    whole = matrix[...]
    top = whole.astype(BF16)
    high_ref[...] = top
    low_ref[...] = (whole - top.astype(F32)).astype(BF16)


def product_kernel(owners, amp_from, amp_self, res_to, operator_high, operator_low, amplitudes, *rest):
    arrived, outs = dict(zip(class_order(owners), rest[: owners - 1])), rest[owners - 1 : 2 * owners - 1]
    own, high, low, totals, sems = rest[2 * owners - 1 :]
    rows, columns = high.shape

    def fetch(k):
        source = amplitudes.at[amp_self[k]]
        return pltpu.make_async_copy(source, own.at[k], sems.at[k])

    def split(d, k):
        g = amp_from[d * CAP + k]

        @pl.when(g >= 0)
        def _():
            if d == 0:
                fetch(k).wait()
                values = own[k]
            else:
                values = arrived[d][k]
            top = values.astype(BF16)
            spot = pl.ds(pl.multiple_of(g * TW, TW), TW)
            high[spot, :] = top
            low[spot, :] = (values - top.astype(F32)).astype(BF16)

    for k in range(CAP):
        pl.when(amp_from[k] >= 0)(fetch(k).start)
    for d in range(owners - 1, -1, -1):
        for k in range(CAP):
            split(d, k)
    step = min(rows, 8 * TW)

    @pl.loop(0, rows // step)
    def _(i):
        here = pl.ds(pl.multiple_of(i * step, step), step)
        total = jnp.dot(operator_high[here, :], low[...], preferred_element_type=F32)
        total += jnp.dot(operator_low[here, :], high[...], preferred_element_type=F32)
        total += jnp.dot(operator_high[here, :], high[...], preferred_element_type=F32)
        for c in range(columns // 128):
            totals[c, here, :] = total[:, c * 128 : (c + 1) * 128]

    for d in range(owners):
        for k in range(CAP):
            g = res_to[d * CAP + k]

            @pl.when(g >= 0)
            def _():
                for c in range(columns // 128):
                    outs[d][k, :, c * 128 : (c + 1) * 128] = totals[c, pl.ds(g, TW, stride=rows // TW), :]


def final_kernel(owners, res_from, res_first, res_last, inverse, *rest):
    arrived, (_, out, sums, sems) = rest[:owners], rest[-4:]
    spots = [(at, k, d * CAP + k) for at, d in enumerate([0] + class_order(owners)) for k in range(CAP)]

    def write(spot):
        source = sums.at[jnp.maximum(res_first[spot], 0)]
        return pltpu.make_async_copy(source, out.at[jnp.maximum(res_from[spot], 0)], sems.at[spot])

    for at, k, spot in spots:
        first = res_first[spot]

        @pl.when(first == spot)
        def _():
            sums[spot] = arrived[at][k] * inverse[spot]

        @pl.when((first >= 0) & (first != spot))
        def _():
            sums[first] = sums[first] + arrived[at][k] * inverse[spot]

        pl.when(res_last[spot] == 1)(write(spot).start)
    for _, _, spot in spots:
        pl.when(res_last[spot] == 1)(write(spot).wait)


def local(
    tasks,
    task_count,
    integrals,
    amplitudes,
    amp_slot,
    need_amp,
    res_slot,
    needed_residual_tiles,
    pair_energy,
    virt_energy,
    window_energy,
):
    owners = lax.axis_size("tile")
    me = lax.axis_index("tile").astype(jnp.int32)
    per_amp, _, row_count = amplitudes.shape
    per_res = res_slot.shape[0] // owners
    list_length = need_amp.shape[0]
    tile_count = virt_energy.shape[0] // TW
    slots = list_length * list_length
    task_slots = tasks.shape[1]

    amplitudes = pltpu.with_memory_space_constraint(amplitudes, pltpu.HBM)
    integrals = pltpu.with_memory_space_constraint(integrals, pltpu.HBM)
    me_ref = me.reshape(1)
    in_hbm = functools.partial(pltpu.with_memory_space_constraint, memory_space=pltpu.HBM)
    spread = pl.pallas_call(
        functools.partial(spread_kernel, list_length),
        out_shape=pltpu.VMEM((owners * 2 * list_length // 128, 128), jnp.int32),
        in_specs=[SMEM_SPEC] * 4,
        out_specs=VMEM_SPEC,
        compiler_params=params(),
        cost_estimate=cost(0, owners * 2 * list_length * 4),
        name="spread_lists",
    )(me_ref, in_hbm(need_amp), in_hbm(needed_residual_tiles), in_hbm(amp_slot))
    lists = lax.psum(spread, "tile").reshape(-1)
    order = class_order(owners)

    def exchange(buffers, classes):
        return [
            in_vmem(lax.ppermute(buffer, "tile", [(i, i ^ d) for i in range(owners)]))
            for buffer, d in zip(buffers, classes)
        ]

    piece = pltpu.VMEM((CAP, TW, row_count), F32)
    fetched = []
    for classes in order[:2], order[2:]:
        packed = pl.pallas_call(
            functools.partial(pack_kernel, classes, list_length, per_amp),
            out_shape=[piece] * len(classes),
            in_specs=[SMEM_SPEC] * 2 + [HBM_SPEC],
            out_specs=[VMEM_SPEC] * len(classes),
            scratch_shapes=[
                pltpu.SMEM((len(classes) * CAP + 1,), jnp.int32),
                pltpu.SemaphoreType.DMA((len(classes) * CAP,)),
            ],
            compiler_params=params(),
            cost_estimate=cost(0, len(classes) * CAP * TW * row_count * 4),
            name="pack_tiles",
        )(me_ref, lists, amplitudes)
        fetched += exchange(packed, classes)

    virt = in_vmem(jnp.broadcast_to(virt_energy.reshape(tile_count, TW, 1), (tile_count, TW, 128)))
    pair = in_vmem(pair_energy.reshape(1, row_count))
    small = pltpu.SMEM((owners * CAP + 1,), jnp.int32)
    *maps, inverse = pl.pallas_call(
        functools.partial(maps_kernel, owners, per_amp, per_res),
        out_shape=[small, pltpu.SMEM((CAP + 1,), jnp.int32), small, small, small, small]
        + [pltpu.VMEM((owners * CAP, TW, row_count), F32)],
        in_specs=[SMEM_SPEC] * 4 + [VMEM_SPEC] * 2,
        out_specs=[SMEM_SPEC] * 6 + [VMEM_SPEC],
        scratch_shapes=[
            pltpu.SMEM((owners * CAP + 1,), jnp.int32),
            pltpu.SMEM((owners,), jnp.int32),
            pltpu.SMEM((per_res + 1,), jnp.int32),
        ],
        compiler_params=params(),
        cost_estimate=cost(0, owners * CAP * TW * row_count * 4),
        name="list_maps",
    )(me_ref, lists, res_slot, window_energy, pair, virt)
    amp_from, amp_self, res_to, res_from, res_first, res_last = (
        pltpu.with_memory_space_constraint(x, pltpu.SMEM) for x in maps
    )
    inverse = in_vmem(inverse)
    block = 1024
    steps = TW * TW // block
    depth = list_length * TW
    operator_rows = depth // steps
    blank_rows = per_res * TW // steps
    keep = depth <= 1024
    operator = pltpu.VMEM((depth, depth), BF16) if keep else jax.ShapeDtypeStruct((depth, depth), BF16)
    operator_high, operator_low, blank = pl.pallas_call(
        functools.partial(sum_kernel, list_length),
        grid=(steps,),
        out_shape=[operator, operator, jax.ShapeDtypeStruct((per_res * TW, row_count), F32)],
        in_specs=[
            SMEM_SPEC,
            pl.BlockSpec((2, task_slots), lambda i: (0, 0)),
            pl.BlockSpec((task_slots, block), lambda i: (0, i)),
        ],
        out_specs=[
            pl.BlockSpec((operator_rows, depth), lambda i: (i, 0)),
            pl.BlockSpec((operator_rows, depth), lambda i: (i, 0)),
            pl.BlockSpec((blank_rows, row_count), lambda i: (i, 0)),
        ],
        scratch_shapes=[
            pltpu.VMEM((slots, task_slots), BF16),
            pltpu.VMEM((block // (2 * TW), slots, 2 * TW), F32),
            pltpu.VMEM((operator_rows, depth), F32),
        ],
        compiler_params=params(),
        cost_estimate=cost(4 * slots * task_slots * TW * TW, (task_slots + slots) * TW * TW * 4),
        name="sum_integrals",
    )(task_count, tasks, integrals)

    blank = blank.reshape(per_res, TW, row_count)
    if keep:
        operator_high, operator_low = in_vmem(operator_high), in_vmem(operator_low)
    products = pl.pallas_call(
        functools.partial(product_kernel, owners),
        out_shape=[piece] * owners,
        in_specs=[SMEM_SPEC] * 3 + [VMEM_SPEC] * 2 + [HBM_SPEC] + [VMEM_SPEC] * (owners - 1),
        out_specs=[VMEM_SPEC] * owners,
        scratch_shapes=[
            pltpu.VMEM((CAP, TW, row_count), F32),
            pltpu.VMEM((depth, row_count), BF16),
            pltpu.VMEM((depth, row_count), BF16),
            pltpu.VMEM((row_count // 128, depth, 128), F32),
            pltpu.SemaphoreType.DMA((CAP,)),
        ],
        compiler_params=params(),
        cost_estimate=cost(6 * depth * depth * row_count, 4 * depth * (depth + 2 * row_count)),
        name="multiply_tiles",
    )(amp_from, amp_self, res_to, operator_high, operator_low, amplitudes, *fetched)
    returned = [in_vmem(products[0])] + exchange([products[d] for d in order], order)
    return pl.pallas_call(
        functools.partial(final_kernel, owners),
        out_shape=jax.ShapeDtypeStruct((per_res, TW, row_count), F32),
        in_specs=[SMEM_SPEC] * 3 + [VMEM_SPEC] * (1 + owners) + [HBM_SPEC],
        out_specs=HBM_SPEC,
        scratch_shapes=[
            pltpu.VMEM((owners * CAP, TW, row_count), F32),
            pltpu.SemaphoreType.DMA((owners * CAP,)),
        ],
        input_output_aliases={4 + owners: 0},
        compiler_params=params(),
        cost_estimate=cost(0, per_res * TW * row_count * 4),
        name="finish_tiles",
    )(res_from, res_first, res_last, inverse, *returned, blank)


def solution(mesh):
    in_specs = (
        P(None, ("mol", "tile")),
        P(("mol", "tile")),
        P(("mol", "tile"), None),
        P(("mol", "tile"), None, "rep"),
        P("mol"),
        P(("mol", "tile")),
        P("mol"),
        P(("mol", "tile")),
        P(("mol", "rep")),
        P("mol"),
        P("mol"),
    )
    out_specs = P(("mol", "tile"), None, "rep")
    return jax.shard_map(local, mesh=mesh, in_specs=in_specs, out_specs=out_specs, check_vma=False)
```
